256 devices in a mesh: batch: 32 (over z, y), proto: 8 (over x, core).
Axes of the slice: x: 4, y: 4, z: 8, core: 2. Of those that a mesh axis runs over, the one named last changes fastest.
Arguments:
- teacher_feat: bfloat16 [8192, 384], P('batch'), may hold values from -6 to 6
- student_feat: bfloat16 [8192, 384], P('batch'), may hold values from -6 to 6
- teacher_protos: bfloat16 [65536, 384], P('proto'), may hold values from -0.31 to 0.31
- student_protos: bfloat16 [65536, 384], P(('proto', 'batch')), may hold values from -0.31 to 0.31
Outputs:
- loss: float32 [], replicated
- grad_student: float32 [8192, 384], P('batch')
- grad_protos: float32 [65536, 384], P(('proto', 'batch'))
The draws below stay inside these ranges and needn't reach their ends.
All inputs are finite; a program needn't handle non-finite values.
Results may differ from the reference program's by a relative error of at most 0.00095.
The reference program's roundings to bfloat16 on the way count: a program that leaves them out, or rounds other values in their place, can miss the bound.
Values may be sent and summed in bfloat16 or wider, within the bound.
A program may use at most 128 MiB of HBM per device.

```python
import math
import jax
import jax.numpy as jnp
from jax import lax

DIM = 384
PROTOS = 65536
BALANCE_ROUNDS = 3
TOKENS = 8192


centre_count = 64


def shared_centres(key):
    return jax.random.normal(key, (centre_count, DIM), jnp.float32)


def crop_centre_index(key):
    picks = jax.random.split(jax.random.fold_in(key, 101), 2)
    first_pick = jax.random.randint(picks[0], (TOKENS,), 0, centre_count)
    second_pick = jax.random.randint(picks[1], (TOKENS,), 0, centre_count)
    return jnp.minimum(first_pick, second_pick)


def proto_centre_index(key):
    picks = jax.random.split(jax.random.fold_in(key, 202), 2)
    first_pick = jax.random.randint(picks[0], (PROTOS,), 0, centre_count)
    second_pick = jax.random.randint(picks[1], (PROTOS,), 0, centre_count)
    return jnp.maximum(first_pick, second_pick)


def log_spread(key, count, lowest, highest):
    return jnp.exp(jax.random.uniform(key, (count, 1), jnp.float32, math.log(lowest), math.log(highest)))


def draw_teacher_feat(key, part):
    centres = shared_centres(key)
    centre_index = crop_centre_index(key)
    key = jax.random.fold_in(key, 11)
    subkeys = jax.random.split(key, 4)
    closeness = log_spread(subkeys[2], TOKENS, 0.25, 1.6)
    anchored = closeness * jnp.take(centres, centre_index, axis=0)
    jitter_part = jax.random.normal(subkeys[3], (TOKENS, DIM), jnp.float32)
    values = anchored + jitter_part
    return jnp.clip(values, -6.0, 6.0).astype(jnp.bfloat16)


def draw_student_feat(key, part):
    centres = shared_centres(key)
    centre_index = crop_centre_index(key)
    key = jax.random.fold_in(key, 37)
    subkeys = jax.random.split(key, 1)
    position = jnp.arange(TOKENS, dtype=jnp.float32) / max(TOKENS - 1, 1)
    anchored = jnp.take(centres, centre_index, axis=0)
    pull = jnp.exp(math.log(0.2) + position * math.log(15.0))
    jitter_part = jax.random.normal(subkeys[0], (TOKENS, DIM), jnp.float32)
    values = pull[:, None] * anchored + jitter_part
    return jnp.clip(values, -6.0, 6.0).astype(jnp.bfloat16)


def draw_teacher_protos(key, part):
    centres = shared_centres(key)
    centre_index = proto_centre_index(key)
    key = jax.random.fold_in(key, 23)
    subkeys = jax.random.split(key, 4)
    attraction = log_spread(subkeys[2], PROTOS, 0.15, 1.6)
    anchored = attraction * jnp.take(centres, centre_index, axis=0)
    jitter_part = jax.random.normal(subkeys[3], (PROTOS, DIM), jnp.float32)
    values = anchored + jitter_part
    return (0.05 * jnp.clip(values, -6.0, 6.0)).astype(jnp.bfloat16)


def draw_student_protos(key, part):
    centres = shared_centres(key)
    centre_index = proto_centre_index(key)
    key = jax.random.fold_in(key, 41)
    subkeys = jax.random.split(key, 2)
    attraction = log_spread(subkeys[0], PROTOS, 0.5, 1.6)
    anchored = attraction * jnp.take(centres, centre_index, axis=0)
    jitter_part = jax.random.normal(subkeys[1], (PROTOS, DIM), jnp.float32)
    values = anchored + jitter_part
    return (0.05 * jnp.clip(values, -6.0, 6.0)).astype(jnp.bfloat16)


def setup_inputs(seed: int = 0) -> dict:
    streams_of = jax.random.split(jax.random.key(seed), 5)
    teacher_feat = draw_teacher_feat(jax.random.fold_in(streams_of[4], 71), 0)
    student_feat = draw_student_feat(jax.random.fold_in(streams_of[4], 71), 0)
    teacher_protos = draw_teacher_protos(jax.random.fold_in(streams_of[4], 71), 0)
    student_protos = draw_student_protos(jax.random.fold_in(streams_of[4], 71), 0)
    return dict(teacher_feat=teacher_feat, student_feat=student_feat, teacher_protos=teacher_protos, student_protos=student_protos)


EPSILON = 1e-06
TEACHER_TEMP = 0.07
STUDENT_TEMP = 0.1

def unit_rows(values):
    wide = values.astype(jnp.float32)
    length = jnp.sqrt(lax.optimization_barrier(jnp.sum(wide * wide, axis=-1, keepdims=True)) + EPSILON)
    return (wide / length, length)

def cross_rows(left, right):
    return lax.dot_general(left, right, (((1,), (1,)), ((), ())), preferred_element_type=jnp.float32)

def reference(teacher_feat, student_feat, teacher_protos, student_protos):
    teacher_unit = unit_rows(teacher_feat)[0].astype(jnp.bfloat16)
    teacher_assignment = unit_rows(teacher_protos)[0].astype(jnp.bfloat16)
    student_table = unit_rows(student_protos)[0].astype(jnp.bfloat16)
    student_dir, student_len = unit_rows(student_feat)
    student_unit = student_dir.astype(jnp.bfloat16)
    kernel = jnp.exp(cross_rows(teacher_unit, teacher_assignment) / TEACHER_TEMP)
    row_scale = jnp.ones((TOKENS,), jnp.float32)
    col_scale = jnp.ones((PROTOS,), jnp.float32)
    for balance_round in range(BALANCE_ROUNDS):
        col_scale = 1.0 / jnp.dot(row_scale, kernel, precision=lax.Precision.HIGHEST)
        row_scale = 1.0 / jnp.dot(kernel, col_scale, precision=lax.Precision.HIGHEST)
    block_rows = math.gcd(TOKENS, 512)
    blocks = TOKENS // block_rows

    def one_block(carry, index):
        start = index * block_rows
        kern_rows = lax.dynamic_slice_in_dim(kernel, start, block_rows, 0)
        units = lax.dynamic_slice_in_dim(student_unit, start, block_rows, 0)
        scale_factors = lax.dynamic_slice_in_dim(row_scale, start, block_rows, 0)
        student_scores = cross_rows(units, student_table) / STUDENT_TEMP
        exp_logits = jnp.exp(student_scores)
        totals = lax.optimization_barrier(jnp.sum(exp_logits, axis=1))
        weighted_targets = kern_rows * col_scale[None, :]
        cross = lax.optimization_barrier(jnp.sum(weighted_targets * student_scores, axis=1))
        losses = jnp.log(totals) - scale_factors * cross
        target = scale_factors[:, None] * weighted_targets
        score_gradient = ((exp_logits / totals[:, None] - target) / STUDENT_TEMP).astype(jnp.bfloat16)
        grad_unit = jnp.dot(score_gradient, student_table, preferred_element_type=jnp.float32)
        prototype_gradient_matrix = carry + lax.dot_general(score_gradient, units, (((0,), (0,)), ((), ())), preferred_element_type=jnp.float32)
        return (prototype_gradient_matrix, (losses, grad_unit))
    grad_protos, (losses, grad_unit) = lax.scan(one_block, jnp.zeros((PROTOS, DIM), jnp.float32), jnp.arange(blocks, dtype=jnp.int32))
    losses = losses.reshape(TOKENS)
    grad_unit = grad_unit.reshape(TOKENS, DIM)
    loss = jnp.sum(losses) / TOKENS
    grad_student = (grad_unit - student_dir * lax.optimization_barrier(jnp.sum(student_dir * grad_unit, axis=1, keepdims=True))) / student_len
    return (loss, grad_student, grad_protos)
```

```python
import functools
import math

import jax
import jax.numpy as jnp
from jax import lax
from jax.experimental import pallas as pl
from jax.experimental.pallas import tpu as pltpu
from jax.sharding import PartitionSpec as P

MESH = pl.DeviceIdType.MESH
NZ, NY, NX, NC = 8, 4, 4, 2
NP = NX * NC
DIM = 384
BLOCK = 256
CROPS = NY * BLOCK
PROTOS = NZ * BLOCK
ROUNDS = 3
EPSILON = 1e-06
LOG2E = 1.4426950408889634
TEACHER_EXP = LOG2E / 0.07
STUDENT_EXP = LOG2E / 0.1
GAIN = 10.0
F32, BF16 = jnp.float32, jnp.bfloat16
LANES = 128
HALF = DIM // 2


def nt_dot(left, right):
    return lax.dot_general(left, right, (((1,), (1,)), ((), ())), preferred_element_type=F32)


def inverse_length(wide):
    return 1.0 / jnp.sqrt(jnp.sum(wide * wide, axis=-1, keepdims=True) + EPSILON)


def fold8(value):
    rows, lanes = value.shape
    return jnp.sum(value.reshape(rows // 8, 8, lanes), axis=0)


def body(
    tf, sf, sp, tp,
    loss_out, gs_out, gp_out,
    raw, tt, st, tu, su, sut, kern, expo, score, grad, cvec, colacc,
    rowacc, totacc, rcol, acol, bcol,
    zbuf, pbuf, ybuf, plast, ylast,
    gp, rs_right, rs_left, gu, gu_sib, xbuf, yred, lossp, lossy, lossz,
    raw_sem, t_send, t_recv, f_send, f_recv, s_send, s_recv, ring_send, ring_recv,
    z_send, z_recv, p_send, p_recv, y_send, y_recv,
    rs_send, rs_recv, sib_send, sib_recv, x_send, x_recv, yr_send, yr_recv, ag_send, ag_recv,
    lp_send, lp_recv, ly_send, ly_recv, lz_send, lz_recv,
):
    b, p = lax.axis_index("batch"), lax.axis_index("proto")
    z, y = b // NY, b % NY
    x, c = p // NC, p % NC

    def at_z(d):
        return (((z + d) % NZ) * NY + y, p)

    def at_y(d):
        return (z * NY + (y + d) % NY, p)

    def at_x(d):
        return (b, ((x + d) % NX) * NC + c)

    def at_p(d):
        return (b, (p + d) % NP)

    sibling = (b, x * NC + 1 - c)

    def remote(src, dst, send, recv, where):
        return pltpu.make_async_remote_copy(
            src_ref=src, dst_ref=dst, send_sem=send, recv_sem=recv, device_id=where, device_id_type=MESH
        )

    def rows256(index):
        return pl.ds(pl.multiple_of(index * BLOCK, BLOCK), BLOCK)

    pending = []

    def launch(copies):
        for copy in copies:
            copy.start()
        return copies

    def arrive(copies):
        for copy in copies:
            copy.wait_recv()
        pending.extend(copies)

    loads = []
    for j in range(NZ):
        load = pltpu.make_async_copy(
            tp.at[pl.ds(pl.multiple_of((j * NY + y) * BLOCK, BLOCK), BLOCK), :], raw.at[pl.ds(j * BLOCK, BLOCK), :], raw_sem.at[j]
        )
        load.start()
        loads.append(load)
    barrier = pltpu.get_barrier_semaphore()
    partners = (
        [at_z(d) for d in range(1, NZ)] + [at_y(d) for d in range(1, NY)] + [at_p(d) for d in range(1, NP)]
    )
    for where in partners:
        pl.semaphore_signal(barrier, inc=1, device_id=where, device_id_type=MESH)

    def unit_into(src, dst, index):
        wide = src[...].astype(F32)
        dst[rows256(index), :] = (wide * inverse_length(wide)).astype(BF16)

    unit_into(tf, tu, y)
    unit_into(sp, st, z)
    unit_into(sf, su, y)
    pl.semaphore_wait(barrier, len(partners))

    def half_rows(index, part):
        return pl.ds(pl.multiple_of(index * BLOCK + part * (BLOCK // 2), BLOCK // 2), BLOCK // 2)

    t_copies = {}
    for d in (2, 1, 3):
        part = tu.at[half_rows(y, c), :]
        t_copies[d] = remote(part, part, t_send.at[d], t_recv.at[d], at_y(d))
        t_copies[d].start()

    def ring(step):
        right, left = (z - step + 1 + NZ) % NZ, (z + step - 1) % NZ
        if step < 4:
            right_rows, left_rows = rows256(right), rows256(left)
        else:
            right_rows, left_rows = half_rows(right, 0), half_rows(left, 1)
        return launch([
            remote(st.at[right_rows, :], st.at[right_rows, :], ring_send.at[step, 0], ring_recv.at[step, 0], at_z(1)),
            remote(st.at[left_rows, :], st.at[left_rows, :], ring_send.at[step, 1], ring_recv.at[step, 1], at_z(NZ - 1)),
        ])

    ring_copies = ring(1)
    s_copies = launch([
        remote(su.at[rows256(y), :], su.at[rows256(y), :], s_send.at[d], s_recv.at[d], at_y(d)) for d in (2, 1, 3)
    ])

    for load in loads:
        load.wait()

    def table_step(i, _):
        rows = pl.ds(pl.multiple_of(i * 64, 64), 64)
        wide = raw[rows, :].astype(F32)
        tt[rows, :] = (wide * inverse_length(wide)).astype(BF16)
        return 0

    lax.fori_loop(0, PROTOS // 64, table_step, 0)
    colacc[...] = jnp.zeros_like(colacc)

    def kernel_block(index):
        def step(j, _):
            cols = rows256(j)
            value = jnp.exp2(nt_dot(tu[rows256(index), :], tt[cols, :]) * TEACHER_EXP)
            kern[rows256(index), cols] = value
            colacc[:, cols] += fold8(value)
            return 0

        lax.fori_loop(0, NZ, step, 0)

    kernel_block(y)
    forwards = {}

    def forward(d):
        t_copies[d].wait_recv()
        part = tu.at[half_rows((y - d + NY) % NY, c), :]
        forwards[d] = remote(part, part, f_send.at[d], f_recv.at[d], sibling)
        forwards[d].start()

    forward(1)
    forward(3)
    forwards[1].wait_recv()
    kernel_block((y + NY - 1) % NY)
    forwards[3].wait_recv()
    kernel_block((y + NY - 3) % NY)
    forward(2)
    arrive(ring_copies)
    ring_copies = ring(2)
    forwards[2].wait_recv()
    kernel_block((y + NY - 2) % NY)

    def student_block(offset):
        cols = rows256((z + offset + NZ) % NZ)

        def step(i, _):
            rows = rows256(i)
            value = nt_dot(su[rows, :], st[cols, :])
            score[rows, cols] = value
            power = jnp.exp2(value * STUDENT_EXP)
            expo[rows, cols] = power
            totacc[rows, :] += power[:, :LANES] + power[:, LANES:]
            return 0

        lax.fori_loop(0, NY, step, 0)

    def student_crops():
        arrive(s_copies)
        totacc[...] = jnp.zeros_like(totacc)
        for i in range(NY):
            rows = pl.ds(i * BLOCK, BLOCK)
            sut[:, rows] = jnp.transpose(su[rows, :].astype(F32)).astype(BF16)

    def lane_sums(src, dst, base):
        for j in range(CROPS // LANES):
            block = jnp.transpose(src[pl.ds(j * LANES, LANES), :])
            dst[base + j : base + j + 1, :] = jnp.sum(block, axis=0, keepdims=True)

    def spread(values, dst):
        for j in range(CROPS // LANES):
            dst[pl.ds(j * LANES, LANES), :] = jnp.transpose(jnp.broadcast_to(values[j : j + 1, :], (LANES, LANES)))

    groups = PROTOS // LANES

    def column_pass():
        def step(i, acc):
            rows = pl.ds(pl.multiple_of(i * 32, 32), 32)
            scale = rcol[rows, :]
            return tuple(acc[g] + fold8(kern[rows, g * LANES : (g + 1) * LANES] * scale) for g in range(groups))

        acc = lax.fori_loop(0, CROPS // 32, step, tuple(jnp.zeros((8, LANES), F32) for _ in range(groups)))
        for g in range(groups):
            colacc[:, g * LANES : (g + 1) * LANES] = acc[g]

    def row_pass():
        def step(i, _):
            rows = pl.ds(pl.multiple_of(i * 64, 64), 64)
            acc = kern[rows, 0:LANES] * cvec[:, 0:LANES]
            for g in range(1, groups):
                acc += kern[rows, g * LANES : (g + 1) * LANES] * cvec[:, g * LANES : (g + 1) * LANES]
            rowacc[rows, :] = acc
            return 0

        lax.fori_loop(0, CROPS // 64, step, 0)

    def exchange(buf, me, send, recv, order, where):
        return launch([remote(buf.at[me], buf.at[me], send.at[d], recv.at[d], where(d)) for d in order])

    def total_of(buf, count):
        total = buf[0]
        for k in range(1, count):
            total += buf[k]
        return total

    for t in range(ROUNDS):
        if t:
            column_pass()
        sums = jnp.sum(colacc[...], axis=0, keepdims=True)
        for j in range(NZ):
            zbuf[t, z, j : j + 1, :] = sums[:, j * BLOCK : (j + 1) * BLOCK]
        copies = exchange(zbuf.at[t], z, z_send.at[t], z_recv.at[t], (4, 3, 5, 2, 6, 1, 7), at_z)
        if t == 0:
            student_crops()
            student_block(0)
            student_block(-1)
            student_block(1)
        if t == 2:
            arrive(ring_copies)
            student_block(4)
        arrive(copies)
        scale = 1.0 / total_of(zbuf.at[t], NZ)
        for j in range(NZ):
            cvec[:, j * BLOCK : (j + 1) * BLOCK] = scale[j : j + 1, :]
        if t < 2:
            arrive(ring_copies)
            ring_copies = ring(3 + t)
        row_pass()
        last = t == ROUNDS - 1
        pb, yb = (plast, ylast) if last else (pbuf.at[t], ybuf.at[t])
        lane_sums(rowacc, pb.at[p], 0)
        if last:
            lane_sums(totacc, pb.at[p], 8)
        copies = exchange(pb, p, p_send.at[t], p_recv.at[t], (4, 3, 5, 2, 6, 1, 7), at_p)
        if t == 0:
            student_block(-2)
            student_block(2)
        if t == 1:
            student_block(-3)
            student_block(3)
        arrive(copies)
        yb[y] = total_of(pb, NP)
        copies = exchange(yb, y, y_send.at[t], y_recv.at[t], (2, 1, 3), at_y)
        arrive(copies)
        sums = total_of(yb, NY)
        if not last:
            spread(1.0 / sums, rcol)
        else:
            totals = sums[8:16, :]
            spread(GAIN / totals, acol)
            spread(GAIN / sums[0:8, :], bcol)

    def grad_block(offset, cross):
        first = pl.multiple_of(((z + offset) % NZ) * BLOCK, BLOCK)

        def step(i, cross):
            rows = pl.ds(pl.multiple_of(i * 64, 64), 64)
            a, bb = acol[rows, :], bcol[rows, :]
            for h in range(BLOCK // LANES):
                cols = pl.ds(pl.multiple_of(first + h * LANES, LANES), LANES)
                target = kern[rows, cols] * cvec[:, cols] * bb
                grad[rows, cols] = (expo[rows, cols] * a - target).astype(BF16)
                cross += fold8(target * score[rows, cols])
            return cross

        return lax.fori_loop(0, CROPS // 64, step, cross)

    def proto_block(offset):
        cols = rows256((z + offset) % NZ)
        gp[offset] = jnp.dot(sut[...], grad[:, cols], preferred_element_type=F32)

    low, high = pl.ds(0, HALF), pl.ds(HALF, HALF)
    units = [
        (4, low, 4, high), (3, high, 5, low), (3, low, 5, high), (2, high, 6, low),
        (2, low, 6, high), (1, high, 7, low), (1, low, 7, high),
    ]
    unit_copies = {}

    def unit(k):
        ro, rh, lo, lh = units[k]
        if k >= 2:
            arrive(unit_copies[k - 2])
            gp[ro, rh, :] += rs_right[k - 2]
            gp[lo, lh, :] += rs_left[k - 2]
        unit_copies[k] = launch([
            remote(gp.at[ro, rh, :], rs_right.at[k], rs_send.at[k, 0], rs_recv.at[k, 0], at_z(1)),
            remote(gp.at[lo, lh, :], rs_left.at[k], rs_send.at[k, 1], rs_recv.at[k, 1], at_z(NZ - 1)),
        ])

    cross = jnp.zeros((8, LANES), F32)
    cross = grad_block(4, cross)
    proto_block(4)
    unit(0)
    for offset in (3, 5):
        cross = grad_block(offset, cross)
        proto_block(offset)
    unit(1)
    for offset in (2, 6, 1, 7, 0):
        cross = grad_block(offset, cross)

    part_rows = BLOCK // NP

    def crop_step(i, _):
        value = jnp.dot(grad[rows256(i), :], st[...], preferred_element_type=F32)
        gu[i] = value.reshape(NC, NX, part_rows, DIM)
        return 0

    lax.fori_loop(0, NY, crop_step, 0)
    sib = launch([remote(gu.at[:, 1 - c], gu_sib, sib_send.at[0], sib_recv.at[0], sibling)])

    lossp[p] = jnp.log(totals) * (1.0 / (NP * NY)) - cross
    loss_copies = exchange(lossp, p, lp_send, lp_recv, (4, 3, 5, 2, 6, 1, 7), at_p)

    for offset in (2, 6):
        proto_block(offset)
    arrive(sib)
    for k in range(NY):
        gu[k, c] += gu_sib[k]
    x_copies = launch([
        remote(gu.at[:, c, (x + d) % NX], xbuf.at[d], x_send.at[d], x_recv.at[d], at_x(d)) for d in (2, 1, 3)
    ])
    for offset in (1, 7, 0):
        proto_block(offset)
    unit(2)
    arrive(loss_copies)
    lossy[y] = total_of(lossp, NP)
    loss_copies = exchange(lossy, y, ly_send, ly_recv, (2, 1, 3), at_y)
    unit(3)
    arrive(loss_copies)
    lossz[z] = total_of(lossy, NY)
    loss_copies = exchange(lossz, z, lz_send, lz_recv, (4, 3, 5, 2, 6, 1, 7), at_z)
    unit(4)
    arrive(x_copies)
    for k in range(NY):
        gu[k, c, x] = gu[k, c, x] + xbuf[1, k] + xbuf[2, k] + xbuf[3, k]
    y_copies = launch([
        remote(gu.at[(y + d) % NY, c, x], yred.at[d], yr_send.at[d], yr_recv.at[d], at_y(d)) for d in (2, 1, 3)
    ])
    unit(5)
    arrive(loss_copies)
    loss_sum = jnp.sum(total_of(lossz, NZ), keepdims=True)
    loss_out[...] = jnp.broadcast_to(loss_sum * (1.0 / (NZ * NY * BLOCK)), (8, LANES))
    unit(6)
    arrive(y_copies)
    grad_unit = gu[y, c, x] + yred[1] + yred[2] + yred[3]
    mine = pl.ds(pl.multiple_of(c * (BLOCK // 2) + x * part_rows, part_rows), part_rows)
    wide = sf[mine, :].astype(F32)
    inverse = inverse_length(wide)
    direction = wide * inverse
    inner = jnp.sum(direction * grad_unit, axis=-1, keepdims=True)
    gs_out[mine, :] = (grad_unit - direction * inner) * inverse
    ag_copies = launch([
        remote(gs_out.at[mine, :], gs_out.at[mine, :], ag_send.at[d], ag_recv.at[d], at_p(d)) for d in (4, 3, 5, 2, 6, 1, 7)
    ])
    arrive(unit_copies[5])
    arrive(unit_copies[6])
    top = gp[0, low, :] + rs_right[6] + rs_left[5]
    bottom = gp[0, high, :] + rs_right[5] + rs_left[6]
    gp_out[:, low] = jnp.transpose(top)
    gp_out[:, high] = jnp.transpose(bottom)
    arrive(ag_copies)
    for copy in list(t_copies.values()) + list(forwards.values()) + pending:
        copy.wait_send()


def on_device(teacher_feat, student_feat, teacher_protos, student_protos):
    vmem, dma = pltpu.VMEM, pltpu.SemaphoreType.DMA
    part_rows = BLOCK // NP
    scratch = [
        vmem((PROTOS, DIM), BF16), vmem((PROTOS, DIM), BF16), vmem((PROTOS, DIM), BF16),
        vmem((CROPS, DIM), BF16), vmem((CROPS, DIM), BF16), vmem((DIM, CROPS), BF16),
        vmem((CROPS, PROTOS), F32), vmem((CROPS, PROTOS), F32), vmem((CROPS, PROTOS), F32),
        vmem((CROPS, PROTOS), BF16), vmem((1, PROTOS), F32), vmem((8, PROTOS), F32),
        *[vmem((CROPS, LANES), F32) for _ in range(5)],
        vmem((ROUNDS, NZ, NZ, BLOCK), F32), vmem((ROUNDS - 1, NP, 8, LANES), F32), vmem((ROUNDS - 1, NY, 8, LANES), F32),
        vmem((NP, 16, LANES), F32), vmem((NY, 16, LANES), F32),
        vmem((NZ, DIM, BLOCK), F32), vmem((7, HALF, BLOCK), F32), vmem((7, HALF, BLOCK), F32),
        vmem((NY, NC, NX, part_rows, DIM), F32), vmem((NY, NX, part_rows, DIM), F32),
        vmem((NX, NY, part_rows, DIM), F32), vmem((NY, part_rows, DIM), F32),
        vmem((NP, 8, LANES), F32), vmem((NY, 8, LANES), F32), vmem((NZ, 8, LANES), F32),
        dma((NZ,)), dma((NY,)), dma((NY,)), dma((NY,)), dma((NY,)), dma((NY,)), dma((NY,)), dma((5, 2)), dma((5, 2)),
        dma((ROUNDS, NZ)), dma((ROUNDS, NZ)), dma((ROUNDS, NP)), dma((ROUNDS, NP)), dma((ROUNDS, NY)), dma((ROUNDS, NY)),
        dma((7, 2)), dma((7, 2)), dma((1,)), dma((1,)), dma((NX,)), dma((NX,)), dma((NY,)), dma((NY,)), dma((NP,)), dma((NP,)),
        dma((NP,)), dma((NP,)), dma((NY,)), dma((NY,)), dma((NZ,)), dma((NZ,)),
    ]
    whole = pl.BlockSpec(memory_space=pltpu.VMEM)
    loss, grad_student, grad_protos = pl.pallas_call(
        body,
        out_shape=(
            jax.ShapeDtypeStruct((8, LANES), F32),
            jax.ShapeDtypeStruct((BLOCK, DIM), F32),
            jax.ShapeDtypeStruct((BLOCK, DIM), F32),
        ),
        in_specs=[whole, whole, whole, pl.BlockSpec(memory_space=pl.ANY)],
        out_specs=(whole, whole, whole),
        scratch_shapes=scratch,
        compiler_params=pltpu.CompilerParams(
            collective_id=0, has_side_effects=True, vmem_limit_bytes=60 << 20
        ),
        name="sinkhorn_head",
    )(teacher_feat, student_feat, student_protos, teacher_protos)
    return loss[0, 0], grad_student, grad_protos


def solution(mesh):
    in_specs = (P("batch", None), P("batch", None), P("proto", None), P(("proto", "batch"), None))
    out_specs = (P(), P("batch", None), P(("proto", "batch"), None))
    return jax.shard_map(on_device, mesh=mesh, in_specs=in_specs, out_specs=out_specs, check_vma=False)
```

```python
import functools
import math

import jax
import jax.numpy as jnp
from jax import lax
from jax.experimental import pallas as pl
from jax.experimental.pallas import tpu as pltpu
from jax.sharding import PartitionSpec as P

MESH = pl.DeviceIdType.MESH
NZ, NY, NX, NC = 8, 4, 4, 2
NP = NX * NC
NXY = NY * NP
DIM = 384
BLOCK = 256
CROPS = NY * BLOCK
PROTOS = NZ * BLOCK
ROUNDS = 3
EPSILON = 1e-06
LOG2E = 1.4426950408889634
TEACHER_EXP = LOG2E / 0.07
STUDENT_EXP = LOG2E / 0.1
GAIN = 10.0
F32, BF16 = jnp.float32, jnp.bfloat16
LANES = 128
HALF = DIM // 2
PARTS = 2
PIECE = HALF // PARTS
Z_ORDER = (4, 3, 5, 2, 6, 1, 7)
P_ORDER = (4, 3, 5, 2, 6, 1, 7)
XY_ORDER = tuple(e * NP + d for e in (2, 1, 3, 0) for d in (4, 3, 5, 2, 6, 1, 7, 0) if e or d)


def nt_dot(left, right):
    return lax.dot_general(left, right, (((1,), (1,)), ((), ())), preferred_element_type=F32)


def inverse_length(wide):
    return 1.0 / jnp.sqrt(jnp.sum(wide * wide, axis=-1, keepdims=True) + EPSILON)


def fold8(value):
    rows, lanes = value.shape
    return jnp.sum(value.reshape(rows // 8, 8, lanes), axis=0)


def body(
    tf, sf, sp, tp,
    loss_out, gs_out, gp_out,
    raw, tt, st, tu, su, sut, kern, expo, score, grad, cvec, colacc,
    rowacc, totacc, rcol, acol, bcol,
    zbuf, rbuf, rlast,
    gp, rs_right, rs_left, own_right, own_left, first_right, first_left, gu, gu_sib, xbuf, yred, ybuf, xred, lossp, lossz,
    raw_sem, t_send, t_recv, f_send, f_recv, s_send, s_recv, ring_send, ring_recv,
    z_send, z_recv, r_send, r_recv,
    rs_send, rs_recv, sib_send, sib_recv, x_send, x_recv, yr_send, yr_recv, yf_send, yf_recv, xr_send, xr_recv, ag_send, ag_recv,
    lp_send, lp_recv, lz_send, lz_recv,
):
    b, p = lax.axis_index("batch"), lax.axis_index("proto")
    z, y = b // NY, b % NY
    x, c = p // NC, p % NC

    def at_z(d):
        return (((z + d) % NZ) * NY + y, p)

    def at_y(d):
        return (z * NY + (y + d) % NY, p)

    def at_xy(d):
        return (z * NY + (y + d // NP) % NY, (p + d % NP) % NP)

    def at_x(d):
        return (b, ((x + d) % NX) * NC + c)

    def at_p(d):
        return (b, (p + d) % NP)

    sibling = (b, x * NC + 1 - c)

    def remote(src, dst, send, recv, where):
        return pltpu.make_async_remote_copy(
            src_ref=src, dst_ref=dst, send_sem=send, recv_sem=recv, device_id=where, device_id_type=MESH
        )

    def rows256(index):
        return pl.ds(pl.multiple_of(index * BLOCK, BLOCK), BLOCK)

    flight, landed = [], []

    def launch(copies):
        for copy in copies:
            copy.start()
        flight.extend(copies)
        return copies

    def arrive(copies):
        for copy in copies:
            copy.wait_recv()
            flight[:] = [other for other in flight if other is not copy]
        landed.extend(copies)

    loads = []
    for j in range(NZ):
        load = pltpu.make_async_copy(
            tp.at[pl.ds(pl.multiple_of((j * NY + y) * BLOCK, BLOCK), BLOCK), :], raw.at[pl.ds(j * BLOCK, BLOCK), :], raw_sem.at[j]
        )
        load.start()
        loads.append(load)
    barrier = pltpu.get_barrier_semaphore()
    partners = (
        [at_z(d) for d in range(1, NZ)] + [at_xy(d) for d in range(1, NXY)]
    )
    for where in partners:
        pl.semaphore_signal(barrier, inc=1, device_id=where, device_id_type=MESH)

    def unit_into(src, dst, index):
        wide = src[...].astype(F32)
        dst[rows256(index), :] = (wide * inverse_length(wide)).astype(BF16)

    unit_into(tf, tu, y)
    unit_into(sp, st, z)
    pl.semaphore_wait(barrier, len(partners))

    def half_rows(index, part):
        return pl.ds(pl.multiple_of(index * BLOCK + part * (BLOCK // 2), BLOCK // 2), BLOCK // 2)

    t_copies = {}
    for d in (2, 1, 3):
        part = tu.at[half_rows(y, c), :]
        t_copies[d] = launch([remote(part, part, t_send.at[d], t_recv.at[d], at_y(d))])

    def ring(step):
        right, left = (z - step + 1 + NZ) % NZ, (z + step - 1) % NZ
        if step < 4:
            right_rows, left_rows = rows256(right), rows256(left)
        else:
            right_rows, left_rows = half_rows(right, 0), half_rows(left, 1)
        return launch([
            remote(st.at[right_rows, :], st.at[right_rows, :], ring_send.at[step, 0], ring_recv.at[step, 0], at_z(1)),
            remote(st.at[left_rows, :], st.at[left_rows, :], ring_send.at[step, 1], ring_recv.at[step, 1], at_z(NZ - 1)),
        ])

    ring_copies = ring(1)

    unit_into(sf, su, y)

    for load in loads:
        load.wait()

    def table_step(i, _):
        rows = rows256(i)
        wide = raw[rows, :].astype(F32)
        tt[rows, :] = (wide * inverse_length(wide)).astype(BF16)
        return 0

    lax.fori_loop(0, NZ, table_step, 0, unroll=2)
    colacc[...] = jnp.zeros_like(colacc)

    def kernel_block(index):
        def step(j, _):
            cols = rows256(j)
            value = jnp.exp2(nt_dot(tu[rows256(index), :], tt[cols, :]) * TEACHER_EXP)
            kern[rows256(index), cols] = value
            colacc[:, cols] += fold8(value)
            return 0

        lax.fori_loop(0, NZ, step, 0, unroll=True)

    kernel_block(y)
    forwards = {}

    def forward(d):
        arrive(t_copies[d])
        part = tu.at[half_rows((y - d + NY) % NY, c), :]
        forwards[d] = launch([remote(part, part, f_send.at[d], f_recv.at[d], sibling)])

    forward(1)
    forward(3)
    arrive(forwards[1])
    kernel_block((y + NY - 1) % NY)
    arrive(forwards[3])
    kernel_block((y + NY - 3) % NY)
    forward(2)
    s_copies = launch([
        remote(su.at[rows256(y), :], su.at[rows256(y), :], s_send.at[d], s_recv.at[d], at_y(d)) for d in (2, 1, 3)
    ])
    arrive(ring_copies)
    ring_copies = ring(2)
    arrive(forwards[2])
    kernel_block((y + NY - 2) % NY)

    def student_block(offset):
        cols = rows256((z + offset + NZ) % NZ)

        def step(i, _):
            rows = rows256(i)
            value = nt_dot(su[rows, :], st[cols, :])
            score[rows, cols] = value
            power = jnp.exp2(value * STUDENT_EXP)
            expo[rows, cols] = power
            totacc[rows, :] += power[:, :LANES] + power[:, LANES:]
            return 0

        lax.fori_loop(0, NY, step, 0, unroll=True)

    def student_blocks(count, offset_of):
        def step(i, _):
            student_block(offset_of(i))
            return 0

        lax.fori_loop(0, count, step, 0)

    def student_crops():
        arrive(s_copies)
        totacc[...] = jnp.zeros_like(totacc)
        for i in range(NY):
            rows = pl.ds(i * BLOCK, BLOCK)
            sut[:, rows] = jnp.transpose(su[rows, :].astype(F32)).astype(BF16)

    def lane_sums(src, dst, base):
        for j in range(CROPS // LANES):
            block = jnp.transpose(src[pl.ds(j * LANES, LANES), :])
            dst[base + j : base + j + 1, :] = jnp.sum(block, axis=0, keepdims=True)

    def spread(values, dst):
        for j in range(CROPS // LANES):
            dst[pl.ds(j * LANES, LANES), :] = jnp.transpose(jnp.broadcast_to(values[j : j + 1, :], (LANES, LANES)))

    groups = PROTOS // LANES

    def column_pass():
        def step(i, acc):
            rows = pl.ds(pl.multiple_of(i * 32, 32), 32)
            scale = rcol[rows, :]
            return tuple(acc[g] + fold8(kern[rows, g * LANES : (g + 1) * LANES] * scale) for g in range(groups))

        acc = lax.fori_loop(0, CROPS // 32, step, tuple(jnp.zeros((8, LANES), F32) for _ in range(groups)), unroll=4)
        for g in range(groups):
            colacc[:, g * LANES : (g + 1) * LANES] = acc[g]

    def row_pass():
        def step(i, _):
            rows = pl.ds(pl.multiple_of(i * 64, 64), 64)
            acc = kern[rows, 0:LANES] * cvec[:, 0:LANES]
            for g in range(1, groups):
                acc += kern[rows, g * LANES : (g + 1) * LANES] * cvec[:, g * LANES : (g + 1) * LANES]
            rowacc[rows, :] = acc
            return 0

        lax.fori_loop(0, CROPS // 64, step, 0, unroll=4)

    def exchange(buf, me, send, recv, order, where):
        return launch([remote(buf.at[me], buf.at[me], send.at[d], recv.at[d], where(d)) for d in order])

    def total_of(buf, count):
        total = buf[0]
        for k in range(1, count):
            total += buf[k]
        return total

    for t in range(ROUNDS):
        if t:
            column_pass()
        sums = jnp.sum(colacc[...], axis=0, keepdims=True)
        for j in range(NZ):
            zbuf[t, z, j : j + 1, :] = sums[:, j * BLOCK : (j + 1) * BLOCK]
        copies = exchange(zbuf.at[t], z, z_send.at[t], z_recv.at[t], Z_ORDER, at_z)
        if t == 2:
            arrive(ring_copies)
            student_block(4)
        arrive(copies)
        scale = 1.0 / total_of(zbuf.at[t], NZ)
        for j in range(NZ):
            cvec[:, j * BLOCK : (j + 1) * BLOCK] = scale[j : j + 1, :]
        if t < 2:
            arrive(ring_copies)
            ring_copies = ring(3 + t)
        row_pass()
        last = t == ROUNDS - 1
        rb = rlast if last else rbuf.at[t]
        mine = y * NP + p
        lane_sums(rowacc, rb.at[mine], 0)
        if last:
            lane_sums(totacc, rb.at[mine], 8)
        copies = exchange(rb, mine, r_send.at[t], r_recv.at[t], XY_ORDER, at_xy)
        if t == 0:
            student_crops()
            student_blocks(3, lambda i: 7 + i)
        if t == 1:
            student_blocks(4, lambda i: 2 + i + i // 2)
        arrive(copies)
        sums = total_of(rb, NXY)
        if not last:
            spread(1.0 / sums, rcol)
        else:
            totals = sums[8:16, :]
            spread(GAIN / totals, acol)
            spread(GAIN / sums[0:8, :], bcol)

    def grad_rows(offset, first_row, count, cross):
        first = pl.multiple_of(((z + offset) % NZ) * BLOCK, BLOCK)

        def step(i, cross):
            rows = pl.ds(pl.multiple_of(first_row + i * 64, 64), 64)
            a, bb = acol[rows, :], bcol[rows, :]
            for h in range(BLOCK // LANES):
                cols = pl.ds(pl.multiple_of(first + h * LANES, LANES), LANES)
                target = kern[rows, cols] * cvec[:, cols] * bb
                grad[rows, cols] = (expo[rows, cols] * a - target).astype(BF16)
                cross += fold8(target * score[rows, cols])
            return cross

        return lax.fori_loop(0, count // 64, step, cross, unroll=4)

    def grad_blocks(count, offset_of, cross, first_row=0, rows=CROPS):
        return lax.fori_loop(0, count, lambda i, total: grad_rows(offset_of(i), first_row, rows, total), cross)

    def proto_blocks(count, offset_of):
        def step(i, _):
            proto_block(offset_of(i))
            return 0

        lax.fori_loop(0, count, step, 0)

    def proto_block(offset):
        cols = rows256((z + offset) % NZ)
        gp[offset] = jnp.dot(sut[...], grad[:, cols], preferred_element_type=F32)

    units = [
        (4, 0, 4, 1), (3, 1, 5, 0), (3, 0, 5, 1), (2, 1, 6, 0), (2, 0, 6, 1), (1, 1, 7, 0), (1, 0, 7, 1),
    ]
    right_way, left_way = at_z(1), at_z(NZ - 1)
    unit_copies = {}

    def piece(half, part):
        return pl.ds(half * HALF + part * PIECE, PIECE)

    def unit(k):
        ro, rh, lo, lh = units[k]
        for part in range(PARTS):
            at = pl.ds(part * PIECE, PIECE)
            mine_right, mine_left = gp.at[ro, piece(rh, part), :], gp.at[lo, piece(lh, part), :]
            if k < 2:
                own_right[k, at, :] = mine_right[...].astype(BF16)
                own_left[k, at, :] = mine_left[...].astype(BF16)
                pair = [(own_right.at[k, at, :], first_right.at[k, at, :]), (own_left.at[k, at, :], first_left.at[k, at, :])]
            else:
                arrive(unit_copies[k - 2, part])
                before_right, before_left = (first_right, first_left) if k < 4 else (rs_right, rs_left)
                mine_right[...] += before_right[k - 2, at, :].astype(F32)
                mine_left[...] += before_left[k - 2, at, :].astype(F32)
                pair = [(mine_right, rs_right.at[k, at, :]), (mine_left, rs_left.at[k, at, :])]
            unit_copies[k, part] = launch([
                remote(pair[0][0], pair[0][1], rs_send.at[k, part, 0], rs_recv.at[k, part, 0], right_way),
                remote(pair[1][0], pair[1][1], rs_send.at[k, part, 1], rs_recv.at[k, part, 1], left_way),
            ])

    cross = jnp.zeros((8, LANES), F32)
    cross = grad_rows(4, 0, CROPS, cross)
    proto_block(4)
    unit(0)
    cross = grad_blocks(2, lambda i: 3 + 2 * i, cross)
    proto_blocks(2, lambda i: 3 + 2 * i)
    unit(1)

    part_rows = BLOCK // NP
    sib, x_copies, y_copies, y_first = {}, {}, {}, {}

    def block_of(e):
        return (y + e) % NY

    def to_sibling(e):
        return remote(gu.at[block_of(e), 1 - c], gu_sib.at[e], sib_send.at[e], sib_recv.at[e], sibling)

    def crop_step(k, cross):
        e = (2 + 3 * k) % NY
        i = block_of(e)
        cross = grad_blocks(5, lambda n: (6 + n) % NZ, cross, pl.multiple_of(i * BLOCK, BLOCK), BLOCK)
        value = jnp.dot(grad[rows256(i), :], st[...], preferred_element_type=F32)
        gu[i] = value.reshape(NC, NX, part_rows, DIM)
        to_sibling(e).start()
        return cross

    cross = lax.fori_loop(0, NY, crop_step, cross)
    for e in range(NY):
        sib[e] = [to_sibling(e)]
    flight.extend(copies[0] for copies in sib.values())

    upper, lower = pl.ds(0, part_rows // 2), pl.ds(part_rows // 2, part_rows // 2)

    def first_hop(e):
        i = block_of(e)
        arrive(sib[e])
        gu[i, c] += gu_sib[e]
        if e:
            y_first[e] = launch([
                remote(gu.at[i, c, :, lower, :], ybuf.at[e], yf_send.at[e], yf_recv.at[e], at_y(e))
            ])
        x_copies[e] = launch([
            remote(gu.at[i, c, (x + d) % NX, upper, :], xbuf.at[e, d], x_send.at[e, d], x_recv.at[e, d], at_x(d))
            for d in (2, 1, 3)
        ])

    def upper_over_y(e):
        i = block_of(e)
        arrive(x_copies[e])
        gu[i, c, x, upper, :] += xbuf[e, 1] + xbuf[e, 2] + xbuf[e, 3]
        if e:
            y_copies[e] = launch([
                remote(gu.at[i, c, x, upper, :], yred.at[e], yr_send.at[e], yr_recv.at[e], at_y(e))
            ])

    def lower_over_x():
        for e in (2, 1, 3):
            arrive(y_first[e])
        gu[y, c, :, lower, :] += ybuf[1] + ybuf[2] + ybuf[3]
        return launch([
            remote(gu.at[y, c, (x + d) % NX, lower, :], xred.at[d], xr_send.at[d], xr_recv.at[d], at_x(d))
            for d in (2, 1, 3)
        ])

    unit(2)
    for e in (2, 1, 0, 3):
        first_hop(e)
    lossp[mine] = jnp.log(totals) * (1.0 / NXY) - cross
    loss_copies = exchange(lossp, mine, lp_send, lp_recv, XY_ORDER, at_xy)
    proto_blocks(2, lambda i: 2 + 4 * i)
    unit(3)
    proto_blocks(3, lambda i: (7 + i) % NZ)
    arrive(loss_copies)
    lossz[z] = total_of(lossp, NXY)
    loss_copies = exchange(lossz, z, lz_send, lz_recv, Z_ORDER, at_z)
    upper_over_y(2)
    upper_over_y(1)
    unit(4)
    x_last = lower_over_x()
    upper_over_y(0)
    upper_over_y(3)
    unit(5)
    arrive(loss_copies)
    loss_out[...] = total_of(lossz, NZ)
    arrive(x_last)
    for e in (2, 1, 3):
        arrive(y_copies[e])
    gu[y, c, x, upper, :] += yred[1] + yred[2] + yred[3]
    gu[y, c, x, lower, :] += xred[1] + xred[2] + xred[3]
    grad_unit = gu[y, c, x]
    part = pl.ds(pl.multiple_of(c * (BLOCK // 2) + x * part_rows, part_rows), part_rows)
    wide = sf[part, :].astype(F32)
    inverse = inverse_length(wide)
    direction = wide * inverse
    inner = jnp.sum(direction * grad_unit, axis=-1, keepdims=True)
    gs_out[part, :] = (grad_unit - direction * inner) * inverse
    ag_copies = launch([
        remote(gs_out.at[part, :], gs_out.at[part, :], ag_send.at[d], ag_recv.at[d], at_p(d)) for d in P_ORDER
    ])
    unit(6)
    for k in (5, 6):
        for part in range(PARTS):
            arrive(unit_copies[k, part])
            at = pl.ds(part * PIECE, PIECE)
            right_half, left_half = units[k][1], units[k][3]
            gp[0, piece(right_half, part), :] += rs_right[k, at, :]
            gp[0, piece(left_half, part), :] += rs_left[k, at, :]
    gp_out[...] = gp[0]
    arrive(ag_copies)
    for copy in landed:
        copy.wait_send()


def finish(loss_parts, gs, gp, loss_out, gs_out, gp_out, loss_in, gs_in, gp_in, sem):
    copies = [
        pltpu.make_async_copy(gp, gp_in, sem.at[0]),
        pltpu.make_async_copy(gs, gs_in, sem.at[1]),
        pltpu.make_async_copy(loss_parts, loss_in, sem.at[2]),
    ]
    for copy in copies:
        copy.start()
    copies[0].wait()
    gp_out[...] = jnp.transpose(gp_in[...])
    copies[1].wait()
    gs_out[...] = gs_in[...]
    copies[2].wait()
    loss_out[...] = jnp.sum(loss_in[...], keepdims=True) * (1.0 / (NZ * NY * BLOCK))


def on_device(teacher_feat, student_feat, teacher_protos, student_protos):
    vmem, dma = pltpu.VMEM, pltpu.SemaphoreType.DMA
    part_rows = BLOCK // NP
    scratch = [
        vmem((PROTOS, DIM), BF16), vmem((PROTOS, DIM), BF16), vmem((PROTOS, DIM), BF16),
        vmem((CROPS, DIM), BF16), vmem((CROPS, DIM), BF16), vmem((DIM, CROPS), BF16),
        vmem((CROPS, PROTOS), F32), vmem((CROPS, PROTOS), F32), vmem((CROPS, PROTOS), F32),
        vmem((CROPS, PROTOS), BF16), vmem((1, PROTOS), F32), vmem((8, PROTOS), F32),
        *[vmem((CROPS, LANES), F32) for _ in range(5)],
        vmem((ROUNDS, NZ, NZ, BLOCK), F32), vmem((ROUNDS - 1, NXY, 8, LANES), F32), vmem((NXY, 16, LANES), F32),
        vmem((NZ, DIM, BLOCK), F32), vmem((7, HALF, BLOCK), F32), vmem((7, HALF, BLOCK), F32),
        *[vmem((2, HALF, BLOCK), BF16) for _ in range(4)],
        vmem((NY, NC, NX, part_rows, DIM), F32), vmem((NY, NX, part_rows, DIM), F32),
        vmem((NY, NX, part_rows // 2, DIM), F32), vmem((NY, part_rows // 2, DIM), F32),
        vmem((NY, NX, part_rows // 2, DIM), F32), vmem((NX, part_rows // 2, DIM), F32),
        vmem((NXY, 8, LANES), F32), vmem((NZ, 8, LANES), F32),
        dma((NZ,)), dma((NY,)), dma((NY,)), dma((NY,)), dma((NY,)), dma((NY,)), dma((NY,)), dma((5, 2)), dma((5, 2)),
        dma((ROUNDS, NZ)), dma((ROUNDS, NZ)), dma((ROUNDS, NXY)), dma((ROUNDS, NXY)),
        dma((7, PARTS, 2)), dma((7, PARTS, 2)), dma((NY,)), dma((NY,)), dma((NY, NX)), dma((NY, NX)), *[dma((NY,)) for _ in range(4)], dma((NX,)), dma((NX,)), dma((NP,)), dma((NP,)),
        dma((NXY,)), dma((NXY,)), dma((NZ,)), dma((NZ,)),
    ]
    whole, anywhere = pl.BlockSpec(memory_space=pltpu.VMEM), pl.BlockSpec(memory_space=pl.ANY)
    loss, grad_student, grad_protos = pl.pallas_call(
        body,
        out_shape=(
            jax.ShapeDtypeStruct((8, LANES), F32),
            jax.ShapeDtypeStruct((BLOCK, DIM), F32),
            jax.ShapeDtypeStruct((DIM, BLOCK), F32),
        ),
        in_specs=[whole, whole, whole, pl.BlockSpec(memory_space=pl.ANY)],
        out_specs=(whole, whole, whole),
        scratch_shapes=scratch,
        compiler_params=pltpu.CompilerParams(
            collective_id=0, has_side_effects=True, vmem_limit_bytes=60 << 20
        ),
        name="sinkhorn_head",
    )(teacher_feat, student_feat, student_protos, teacher_protos)
    loss, grad_student, grad_protos = pl.pallas_call(
        finish,
        out_shape=(
            jax.ShapeDtypeStruct((1, 1), F32),
            jax.ShapeDtypeStruct((BLOCK, DIM), F32),
            jax.ShapeDtypeStruct((BLOCK, DIM), F32),
        ),
        in_specs=[anywhere, anywhere, anywhere],
        out_specs=(whole, whole, whole),
        scratch_shapes=[vmem((8, LANES), F32), vmem((BLOCK, DIM), F32), vmem((DIM, BLOCK), F32), dma((3,))],
        name="finish",
    )(loss, grad_student, grad_protos)
    return loss.reshape(()), grad_student, grad_protos


def solution(mesh):
    in_specs = (P("batch", None), P("batch", None), P("proto", None), P(("proto", "batch"), None))
    out_specs = (P(), P("batch", None), P(("proto", "batch"), None))
    return jax.shard_map(on_device, mesh=mesh, in_specs=in_specs, out_specs=out_specs, check_vma=False)
```

```python
import functools
import math

import jax
import jax.numpy as jnp
from jax import lax
from jax.experimental import pallas as pl
from jax.experimental.pallas import tpu as pltpu
from jax.sharding import PartitionSpec as P

MESH = pl.DeviceIdType.MESH
NZ, NY, NX, NC = 8, 4, 4, 2
NP = NX * NC
NXY = NY * NP
DIM = 384
BLOCK = 256
CROPS = NY * BLOCK
PROTOS = NZ * BLOCK
ROUNDS = 3
EPSILON = 1e-06
LOG2E = 1.4426950408889634
TEACHER_EXP = LOG2E / 0.07
STUDENT_EXP = LOG2E / 0.1
GAIN = 10.0
F32, BF16 = jnp.float32, jnp.bfloat16
LANES = 128
HALF = DIM // 2
PARTS = 2
PIECE = HALF // PARTS
Z_ORDER = (4, 3, 5, 2, 6, 1, 7)
P_ORDER = (4, 3, 5, 2, 6, 1, 7)
XY_ORDER = tuple(e * NP + d for e in (2, 1, 3, 0) for d in (4, 3, 5, 2, 6, 1, 7, 0) if e or d)


def nt_dot(left, right):
    return lax.dot_general(left, right, (((1,), (1,)), ((), ())), preferred_element_type=F32)


def inverse_length(wide):
    return 1.0 / jnp.sqrt(jnp.sum(wide * wide, axis=-1, keepdims=True) + EPSILON)


def fold8(value):
    rows, lanes = value.shape
    return jnp.sum(value.reshape(rows // 8, 8, lanes), axis=0)


def body(
    tf, sf, sp, tp,
    loss_out, gs_out, gp_out,
    raw, tt, st, tu, su, sut, kern, expo, score, grad, cvec, colacc,
    rowacc, totacc, rcol, acol, bcol,
    zbuf, rbuf, rlast,
    gp, rs_right, rs_left, own_right, own_left, first_right, first_left, gu, gu_sib, xbuf, yred, ybuf, xall, lossp, lossz,
    raw_sem, t_send, t_recv, f_send, f_recv, s_send, s_recv, ring_send, ring_recv,
    z_send, z_recv, r_send, r_recv,
    rs_send, rs_recv, sib_send, sib_recv, x_send, x_recv, yr_send, yr_recv, yf_send, yf_recv, xr_send, xr_recv, low_send, low_recv, ag_send, ag_recv,
    lp_send, lp_recv, lz_send, lz_recv,
):
    b, p = lax.axis_index("batch"), lax.axis_index("proto")
    z, y = b // NY, b % NY
    x, c = p // NC, p % NC

    def at_z(d):
        return (((z + d) % NZ) * NY + y, p)

    def at_y(d):
        return (z * NY + (y + d) % NY, p)

    def at_xy(d):
        return (z * NY + (y + d // NP) % NY, (p + d % NP) % NP)

    def at_x(d):
        return (b, ((x + d) % NX) * NC + c)

    def at_p(d):
        return (b, (p + d) % NP)

    sibling = (b, x * NC + 1 - c)

    def remote(src, dst, send, recv, where):
        return pltpu.make_async_remote_copy(
            src_ref=src, dst_ref=dst, send_sem=send, recv_sem=recv, device_id=where, device_id_type=MESH
        )

    def rows256(index):
        return pl.ds(pl.multiple_of(index * BLOCK, BLOCK), BLOCK)

    flight, landed = [], []

    def launch(copies):
        for copy in copies:
            copy.start()
        flight.extend(copies)
        return copies

    def arrive(copies):
        for copy in copies:
            copy.wait_recv()
            flight[:] = [other for other in flight if other is not copy]
        landed.extend(copies)

    loads = []
    for j in range(NZ):
        load = pltpu.make_async_copy(
            tp.at[pl.ds(pl.multiple_of((j * NY + y) * BLOCK, BLOCK), BLOCK), :], raw.at[pl.ds(j * BLOCK, BLOCK), :], raw_sem.at[j]
        )
        load.start()
        loads.append(load)
    barrier = pltpu.get_barrier_semaphore()
    partners = (
        [at_z(d) for d in range(1, NZ)] + [at_xy(d) for d in range(1, NXY)]
    )
    for where in partners:
        pl.semaphore_signal(barrier, inc=1, device_id=where, device_id_type=MESH)

    def unit_into(src, dst, index):
        wide = src[...].astype(F32)
        dst[rows256(index), :] = (wide * inverse_length(wide)).astype(BF16)

    unit_into(tf, tu, y)
    unit_into(sp, st, z)
    pl.semaphore_wait(barrier, len(partners))

    def half_rows(index, part):
        return pl.ds(pl.multiple_of(index * BLOCK + part * (BLOCK // 2), BLOCK // 2), BLOCK // 2)

    t_copies = {}
    for d in (2, 1, 3):
        part = tu.at[half_rows(y, c), :]
        t_copies[d] = launch([remote(part, part, t_send.at[d], t_recv.at[d], at_y(d))])

    def ring(step):
        right, left = (z - step + 1 + NZ) % NZ, (z + step - 1) % NZ
        if step < 4:
            right_rows, left_rows = rows256(right), rows256(left)
        else:
            right_rows, left_rows = half_rows(right, 0), half_rows(left, 1)
        return launch([
            remote(st.at[right_rows, :], st.at[right_rows, :], ring_send.at[step, 0], ring_recv.at[step, 0], at_z(1)),
            remote(st.at[left_rows, :], st.at[left_rows, :], ring_send.at[step, 1], ring_recv.at[step, 1], at_z(NZ - 1)),
        ])

    ring_copies = ring(1)

    unit_into(sf, su, y)

    for load in loads:
        load.wait()

    def table_step(i, _):
        rows = rows256(i)
        wide = raw[rows, :].astype(F32)
        tt[rows, :] = (wide * inverse_length(wide)).astype(BF16)
        return 0

    lax.fori_loop(0, NZ, table_step, 0, unroll=2)
    colacc[...] = jnp.zeros_like(colacc)

    def kernel_block(index):
        def step(j, _):
            cols = rows256(j)
            value = jnp.exp2(nt_dot(tu[rows256(index), :], tt[cols, :]) * TEACHER_EXP)
            kern[rows256(index), cols] = value
            colacc[:, cols] += fold8(value)
            return 0

        lax.fori_loop(0, NZ, step, 0, unroll=True)

    kernel_block(y)
    forwards = {}

    def forward(d):
        arrive(t_copies[d])
        part = tu.at[half_rows((y - d + NY) % NY, c), :]
        forwards[d] = launch([remote(part, part, f_send.at[d], f_recv.at[d], sibling)])

    forward(1)
    forward(3)
    arrive(forwards[1])
    kernel_block((y + NY - 1) % NY)
    arrive(forwards[3])
    kernel_block((y + NY - 3) % NY)
    forward(2)
    s_copies = launch([
        remote(su.at[rows256(y), :], su.at[rows256(y), :], s_send.at[d], s_recv.at[d], at_y(d)) for d in (2, 1, 3)
    ])
    arrive(ring_copies)
    ring_copies = ring(2)
    arrive(forwards[2])
    kernel_block((y + NY - 2) % NY)

    def student_block(offset):
        cols = rows256((z + offset + NZ) % NZ)

        def step(i, _):
            rows = rows256(i)
            value = nt_dot(su[rows, :], st[cols, :])
            score[rows, cols] = value
            power = jnp.exp2(value * STUDENT_EXP)
            expo[rows, cols] = power
            totacc[rows, :] += power[:, :LANES] + power[:, LANES:]
            return 0

        lax.fori_loop(0, NY, step, 0, unroll=True)

    def student_blocks(count, offset_of):
        def step(i, _):
            student_block(offset_of(i))
            return 0

        lax.fori_loop(0, count, step, 0)

    def student_crops():
        arrive(s_copies)
        totacc[...] = jnp.zeros_like(totacc)
        for i in range(NY):
            rows = pl.ds(i * BLOCK, BLOCK)
            sut[:, rows] = jnp.transpose(su[rows, :].astype(F32)).astype(BF16)

    def lane_sums(src, dst, base):
        for j in range(CROPS // LANES):
            block = jnp.transpose(src[pl.ds(j * LANES, LANES), :])
            dst[base + j : base + j + 1, :] = jnp.sum(block, axis=0, keepdims=True)

    def spread(values, dst):
        for j in range(CROPS // LANES):
            dst[pl.ds(j * LANES, LANES), :] = jnp.transpose(jnp.broadcast_to(values[j : j + 1, :], (LANES, LANES)))

    groups = PROTOS // LANES

    def column_pass():
        def step(i, acc):
            rows = pl.ds(pl.multiple_of(i * 32, 32), 32)
            scale = rcol[rows, :]
            return tuple(acc[g] + fold8(kern[rows, g * LANES : (g + 1) * LANES] * scale) for g in range(groups))

        acc = lax.fori_loop(0, CROPS // 32, step, tuple(jnp.zeros((8, LANES), F32) for _ in range(groups)), unroll=4)
        for g in range(groups):
            colacc[:, g * LANES : (g + 1) * LANES] = acc[g]

    def row_pass():
        def step(i, _):
            rows = pl.ds(pl.multiple_of(i * 64, 64), 64)
            acc = kern[rows, 0:LANES] * cvec[:, 0:LANES]
            for g in range(1, groups):
                acc += kern[rows, g * LANES : (g + 1) * LANES] * cvec[:, g * LANES : (g + 1) * LANES]
            rowacc[rows, :] = acc
            return 0

        lax.fori_loop(0, CROPS // 64, step, 0, unroll=4)

    def exchange(buf, me, send, recv, order, where):
        return launch([remote(buf.at[me], buf.at[me], send.at[d], recv.at[d], where(d)) for d in order])

    def total_of(buf, count):
        total = buf[0]
        for k in range(1, count):
            total += buf[k]
        return total

    for t in range(ROUNDS):
        if t:
            column_pass()
        sums = jnp.sum(colacc[...], axis=0, keepdims=True)
        for j in range(NZ):
            zbuf[t, z, j : j + 1, :] = sums[:, j * BLOCK : (j + 1) * BLOCK]
        copies = exchange(zbuf.at[t], z, z_send.at[t], z_recv.at[t], Z_ORDER, at_z)
        if t == 2:
            arrive(ring_copies)
            student_block(4)
        arrive(copies)
        scale = 1.0 / total_of(zbuf.at[t], NZ)
        for j in range(NZ):
            cvec[:, j * BLOCK : (j + 1) * BLOCK] = scale[j : j + 1, :]
        if t < 2:
            arrive(ring_copies)
            ring_copies = ring(3 + t)
        row_pass()
        last = t == ROUNDS - 1
        rb = rlast if last else rbuf.at[t]
        mine = y * NP + p
        lane_sums(rowacc, rb.at[mine], 0)
        if last:
            lane_sums(totacc, rb.at[mine], 8)
        copies = exchange(rb, mine, r_send.at[t], r_recv.at[t], XY_ORDER, at_xy)
        if t == 0:
            student_crops()
            student_blocks(3, lambda i: 7 + i)
        if t == 1:
            student_blocks(4, lambda i: 2 + i + i // 2)
        arrive(copies)
        sums = total_of(rb, NXY)
        if not last:
            spread(1.0 / sums, rcol)
        else:
            totals = sums[8:16, :]
            spread(GAIN / totals, acol)
            spread(GAIN / sums[0:8, :], bcol)

    def grad_rows(offset, first_row, count, cross):
        first = pl.multiple_of(((z + offset) % NZ) * BLOCK, BLOCK)

        def step(i, cross):
            rows = pl.ds(pl.multiple_of(first_row + i * 64, 64), 64)
            a, bb = acol[rows, :], bcol[rows, :]
            for h in range(BLOCK // LANES):
                cols = pl.ds(pl.multiple_of(first + h * LANES, LANES), LANES)
                target = kern[rows, cols] * cvec[:, cols] * bb
                grad[rows, cols] = (expo[rows, cols] * a - target).astype(BF16)
                cross += fold8(target * score[rows, cols])
            return cross

        return lax.fori_loop(0, count // 64, step, cross, unroll=4)

    def grad_blocks(count, offset_of, cross, first_row=0, rows=CROPS):
        return lax.fori_loop(0, count, lambda i, total: grad_rows(offset_of(i), first_row, rows, total), cross)

    def proto_blocks(count, offset_of):
        def step(i, _):
            proto_block(offset_of(i))
            return 0

        lax.fori_loop(0, count, step, 0)

    def proto_block(offset):
        cols = rows256((z + offset) % NZ)
        gp[offset] = jnp.dot(sut[...], grad[:, cols], preferred_element_type=F32)

    units = [
        (4, 0, 4, 1), (3, 1, 5, 0), (3, 0, 5, 1), (2, 1, 6, 0), (2, 0, 6, 1), (1, 1, 7, 0), (1, 0, 7, 1),
    ]
    right_way, left_way = at_z(1), at_z(NZ - 1)
    unit_copies = {}

    def piece(half, part):
        return pl.ds(half * HALF + part * PIECE, PIECE)

    def unit(k):
        ro, rh, lo, lh = units[k]
        for part in range(PARTS):
            at = pl.ds(part * PIECE, PIECE)
            mine_right, mine_left = gp.at[ro, piece(rh, part), :], gp.at[lo, piece(lh, part), :]
            if k < 2:
                own_right[k, at, :] = mine_right[...].astype(BF16)
                own_left[k, at, :] = mine_left[...].astype(BF16)
                pair = [(own_right.at[k, at, :], first_right.at[k, at, :]), (own_left.at[k, at, :], first_left.at[k, at, :])]
            else:
                arrive(unit_copies[k - 2, part])
                before_right, before_left = (first_right, first_left) if k < 4 else (rs_right, rs_left)
                mine_right[...] += before_right[k - 2, at, :].astype(F32)
                mine_left[...] += before_left[k - 2, at, :].astype(F32)
                pair = [(mine_right, rs_right.at[k, at, :]), (mine_left, rs_left.at[k, at, :])]
            unit_copies[k, part] = launch([
                remote(pair[0][0], pair[0][1], rs_send.at[k, part, 0], rs_recv.at[k, part, 0], right_way),
                remote(pair[1][0], pair[1][1], rs_send.at[k, part, 1], rs_recv.at[k, part, 1], left_way),
            ])

    cross = jnp.zeros((8, LANES), F32)
    cross = grad_rows(4, 0, CROPS, cross)
    proto_block(4)
    unit(0)
    cross = grad_blocks(2, lambda i: 3 + 2 * i, cross)
    proto_blocks(2, lambda i: 3 + 2 * i)
    unit(1)

    part_rows = BLOCK // NP
    sib, x_copies, y_copies, y_first = {}, {}, {}, {}

    def block_of(e):
        return (y + e) % NY

    def to_sibling(e):
        return remote(gu.at[block_of(e), 1 - c], gu_sib.at[e], sib_send.at[e], sib_recv.at[e], sibling)

    def crop_step(k, cross):
        e = (2 + 3 * k) % NY
        i = block_of(e)
        cross = grad_blocks(5, lambda n: (6 + n) % NZ, cross, pl.multiple_of(i * BLOCK, BLOCK), BLOCK)
        value = jnp.dot(grad[rows256(i), :], st[...], preferred_element_type=F32)
        gu[i] = value.reshape(NC, NX, part_rows, DIM)
        to_sibling(e).start()
        return cross

    cross = lax.fori_loop(0, 2, crop_step, cross)
    unit(2)
    cross = lax.fori_loop(2, NY, crop_step, cross)
    proto_blocks(2, lambda i: 2 + 4 * i)
    unit(3)
    for e in range(NY):
        sib[e] = [to_sibling(e)]
    flight.extend(copies[0] for copies in sib.values())

    upper, lower = pl.ds(0, part_rows // 2), pl.ds(part_rows // 2, part_rows // 2)

    def first_hop(e):
        i = block_of(e)
        arrive(sib[e])
        gu[i, c] += gu_sib[e]
        if e:
            y_first[e] = launch([
                remote(gu.at[i, c, :, lower, :], ybuf.at[e], yf_send.at[e], yf_recv.at[e], at_y(e))
            ])
        x_copies[e] = launch([
            remote(gu.at[i, c, (x + d) % NX, upper, :], xbuf.at[e, d], x_send.at[e, d], x_recv.at[e, d], at_x(d))
            for d in (2, 1, 3)
        ])

    def upper_over_y(e):
        i = block_of(e)
        arrive(x_copies[e])
        gu[i, c, x, upper, :] += xbuf[e, 1] + xbuf[e, 2] + xbuf[e, 3]
        if e:
            y_copies[e] = launch([
                remote(gu.at[i, c, x, upper, :], yred.at[e], yr_send.at[e], yr_recv.at[e], at_y(e))
            ])

    def lower_over_x():
        for e in (2, 1, 3):
            arrive(y_first[e])
        xall[x] = gu[y, c, :, lower, :] + ybuf[1] + ybuf[2] + ybuf[3]
        return exchange(xall, x, xr_send, xr_recv, (2, 1, 3), at_x)

    def finished(rows, grad_unit):
        wide = sf[rows, :].astype(F32)
        inverse = inverse_length(wide)
        direction = wide * inverse
        inner = jnp.sum(direction * grad_unit, axis=-1, keepdims=True)
        gs_out[rows, :] = (grad_unit - direction * inner) * inverse

    def half_part(k, half):
        size = part_rows // 2
        return pl.ds(pl.multiple_of(c * (BLOCK // 2) + k * part_rows + half * size, size), size)

    for e in (2, 1, 0, 3):
        first_hop(e)
    proto_blocks(3, lambda i: (7 + i) % NZ)
    lossp[mine] = jnp.log(totals) * (1.0 / NXY) - cross
    loss_copies = exchange(lossp, mine, lp_send, lp_recv, XY_ORDER, at_xy)
    unit(4)
    unit(5)
    x_last = lower_over_x()
    for e in (2, 1, 0, 3):
        upper_over_y(e)
    arrive(loss_copies)
    lossz[z] = total_of(lossp, NXY)
    loss_copies = exchange(lossz, z, lz_send, lz_recv, Z_ORDER, at_z)
    unit(6)
    for e in (2, 1, 3):
        arrive(y_copies[e])
    part = half_part(x, 0)
    finished(part, gu[y, c, x, upper, :] + yred[1] + yred[2] + yred[3])
    ag_copies = launch([
        remote(gs_out.at[part, :], gs_out.at[part, :], ag_send.at[d], ag_recv.at[d], at_p(d)) for d in P_ORDER
    ])
    arrive(x_last)
    low_copies = []
    for k in range(NX):
        rows = half_part(k, 1)
        finished(rows, xall[0, k] + xall[1, k] + xall[2, k] + xall[3, k])
        low_copies += launch([remote(gs_out.at[rows, :], gs_out.at[rows, :], low_send.at[k], low_recv.at[k], sibling)])
    for k in (5, 6):
        for part in range(PARTS):
            arrive(unit_copies[k, part])
            at = pl.ds(part * PIECE, PIECE)
            right_half, left_half = units[k][1], units[k][3]
            gp[0, piece(right_half, part), :] += rs_right[k, at, :]
            gp[0, piece(left_half, part), :] += rs_left[k, at, :]
    gp_out[...] = gp[0]
    arrive(loss_copies)
    loss_out[...] = total_of(lossz, NZ)
    arrive(low_copies)
    arrive(ag_copies)
    for copy in landed:
        copy.wait_send()


def finish(loss_parts, gs, gp, loss_out, gs_out, gp_out, loss_in, gs_in, gp_in, sem):
    copies = [
        pltpu.make_async_copy(gp, gp_in, sem.at[0]),
        pltpu.make_async_copy(gs, gs_in, sem.at[1]),
        pltpu.make_async_copy(loss_parts, loss_in, sem.at[2]),
    ]
    for copy in copies:
        copy.start()
    copies[0].wait()
    gp_out[...] = jnp.transpose(gp_in[...])
    copies[1].wait()
    gs_out[...] = gs_in[...]
    copies[2].wait()
    loss_out[...] = jnp.sum(loss_in[...], keepdims=True) * (1.0 / (NZ * NY * BLOCK))


def on_device(teacher_feat, student_feat, teacher_protos, student_protos):
    vmem, dma = pltpu.VMEM, pltpu.SemaphoreType.DMA
    part_rows = BLOCK // NP
    scratch = [
        vmem((PROTOS, DIM), BF16), vmem((PROTOS, DIM), BF16), vmem((PROTOS, DIM), BF16),
        vmem((CROPS, DIM), BF16), vmem((CROPS, DIM), BF16), vmem((DIM, CROPS), BF16),
        vmem((CROPS, PROTOS), F32), vmem((CROPS, PROTOS), F32), vmem((CROPS, PROTOS), F32),
        vmem((CROPS, PROTOS), BF16), vmem((1, PROTOS), F32), vmem((8, PROTOS), F32),
        *[vmem((CROPS, LANES), F32) for _ in range(5)],
        vmem((ROUNDS, NZ, NZ, BLOCK), F32), vmem((ROUNDS - 1, NXY, 8, LANES), F32), vmem((NXY, 16, LANES), F32),
        vmem((NZ, DIM, BLOCK), F32), vmem((7, HALF, BLOCK), F32), vmem((7, HALF, BLOCK), F32),
        *[vmem((2, HALF, BLOCK), BF16) for _ in range(4)],
        vmem((NY, NC, NX, part_rows, DIM), F32), vmem((NY, NX, part_rows, DIM), F32),
        vmem((NY, NX, part_rows // 2, DIM), F32), vmem((NY, part_rows // 2, DIM), F32),
        vmem((NY, NX, part_rows // 2, DIM), F32), vmem((NX, NX, part_rows // 2, DIM), F32),
        vmem((NXY, 8, LANES), F32), vmem((NZ, 8, LANES), F32),
        dma((NZ,)), dma((NY,)), dma((NY,)), dma((NY,)), dma((NY,)), dma((NY,)), dma((NY,)), dma((5, 2)), dma((5, 2)),
        dma((ROUNDS, NZ)), dma((ROUNDS, NZ)), dma((ROUNDS, NXY)), dma((ROUNDS, NXY)),
        dma((7, PARTS, 2)), dma((7, PARTS, 2)), dma((NY,)), dma((NY,)), dma((NY, NX)), dma((NY, NX)), *[dma((NY,)) for _ in range(4)], *[dma((NX,)) for _ in range(4)], dma((NP,)), dma((NP,)),
        dma((NXY,)), dma((NXY,)), dma((NZ,)), dma((NZ,)),
    ]
    whole, anywhere = pl.BlockSpec(memory_space=pltpu.VMEM), pl.BlockSpec(memory_space=pl.ANY)
    loss, grad_student, grad_protos = pl.pallas_call(
        body,
        out_shape=(
            jax.ShapeDtypeStruct((8, LANES), F32),
            jax.ShapeDtypeStruct((BLOCK, DIM), F32),
            jax.ShapeDtypeStruct((DIM, BLOCK), F32),
        ),
        in_specs=[whole, whole, whole, pl.BlockSpec(memory_space=pl.ANY)],
        out_specs=(whole, whole, whole),
        scratch_shapes=scratch,
        compiler_params=pltpu.CompilerParams(
            collective_id=0, has_side_effects=True, vmem_limit_bytes=60 << 20
        ),
        name="sinkhorn_head",
    )(teacher_feat, student_feat, student_protos, teacher_protos)
    loss, grad_student, grad_protos = pl.pallas_call(
        finish,
        out_shape=(
            jax.ShapeDtypeStruct((1, 1), F32),
            jax.ShapeDtypeStruct((BLOCK, DIM), F32),
            jax.ShapeDtypeStruct((BLOCK, DIM), F32),
        ),
        in_specs=[anywhere, anywhere, anywhere],
        out_specs=(whole, whole, whole),
        scratch_shapes=[vmem((8, LANES), F32), vmem((BLOCK, DIM), F32), vmem((DIM, BLOCK), F32), dma((3,))],
        name="finish",
    )(loss, grad_student, grad_protos)
    return loss.reshape(()), grad_student, grad_protos


def solution(mesh):
    in_specs = (P("batch", None), P("batch", None), P("proto", None), P(("proto", "batch"), None))
    out_specs = (P(), P("batch", None), P(("proto", "batch"), None))
    return jax.shard_map(on_device, mesh=mesh, in_specs=in_specs, out_specs=out_specs, check_vma=False)
```

```python
import functools
import math

import jax
import jax.numpy as jnp
from jax import lax
from jax.experimental import pallas as pl
from jax.experimental.pallas import tpu as pltpu
from jax.sharding import PartitionSpec as P

MESH = pl.DeviceIdType.MESH
NZ, NY, NX, NC = 8, 4, 4, 2
NP = NX * NC
NXY = NY * NP
DIM = 384
BLOCK = 256
CROPS = NY * BLOCK
PROTOS = NZ * BLOCK
ROUNDS = 3
EPSILON = 1e-06
LOG2E = 1.4426950408889634
TEACHER_EXP = LOG2E / 0.07
STUDENT_EXP = LOG2E / 0.1
GAIN = 10.0
F32, BF16 = jnp.float32, jnp.bfloat16
LANES = 128
HALF = DIM // 2
PARTS = 2
PIECE = HALF // PARTS
Z_ORDER = (4, 3, 5, 2, 6, 1, 7)
P_ORDER = (4, 3, 5, 2, 6, 1, 7)
XY_ORDER = tuple(e * NP + d for e in (2, 1, 3, 0) for d in (4, 3, 5, 2, 6, 1, 7, 0) if e or d)


def nt_dot(left, right):
    return lax.dot_general(left, right, (((1,), (1,)), ((), ())), preferred_element_type=F32)


def inverse_length(wide):
    return 1.0 / jnp.sqrt(jnp.sum(wide * wide, axis=-1, keepdims=True) + EPSILON)


def fold8(value):
    rows, lanes = value.shape
    return jnp.sum(value.reshape(rows // 8, 8, lanes), axis=0)


def body(
    tf_in, sf_in, sp_in, tp,
    loss_out, gs_out, gp_out,
    tf, sf, sp, raw, tt, st, tu, su, sut, kern, expo, score, grad, cvec, colacc,
    rowacc, totacc, rcol, acol, bcol,
    zbuf, rbuf, rlast,
    gp, rs_right, rs_left, own_right, own_left, first_right, first_left, gu, gu_sib, xbuf, yred, ybuf, xall, lossp, lossz,
    in_sem, raw_sem, t_send, t_recv, f_send, f_recv, s_send, s_recv, ring_send, ring_recv,
    z_send, z_recv, r_send, r_recv,
    rs_send, rs_recv, sib_send, sib_recv, x_send, x_recv, yr_send, yr_recv, yf_send, yf_recv, xr_send, xr_recv, low_send, low_recv, ag_send, ag_recv,
    lp_send, lp_recv, lz_send, lz_recv,
):
    b, p = lax.axis_index("batch"), lax.axis_index("proto")
    z, y = b // NY, b % NY
    x, c = p // NC, p % NC

    def at_z(d):
        return (((z + d) % NZ) * NY + y, p)

    def at_y(d):
        return (z * NY + (y + d) % NY, p)

    def at_xy(d):
        return (z * NY + (y + d // NP) % NY, (p + d % NP) % NP)

    def at_x(d):
        return (b, ((x + d) % NX) * NC + c)

    def at_p(d):
        return (b, (p + d) % NP)

    sibling = (b, x * NC + 1 - c)

    def remote(src, dst, send, recv, where):
        return pltpu.make_async_remote_copy(
            src_ref=src, dst_ref=dst, send_sem=send, recv_sem=recv, device_id=where, device_id_type=MESH
        )

    def rows256(index):
        return pl.ds(pl.multiple_of(index * BLOCK, BLOCK), BLOCK)

    flight, landed = [], []

    def launch(copies):
        for copy in copies:
            copy.start()
        flight.extend(copies)
        return copies

    def arrive(copies):
        for copy in copies:
            copy.wait_recv()
            flight[:] = [other for other in flight if other is not copy]
        landed.extend(copies)

    barrier = pltpu.get_barrier_semaphore()
    partners = (
        [at_z(d) for d in range(1, NZ)] + [at_xy(d) for d in range(1, NXY)]
    )
    for where in partners:
        pl.semaphore_signal(barrier, inc=1, device_id=where, device_id_type=MESH)
    own = [
        pltpu.make_async_copy(src, dst, in_sem.at[k]) for k, (src, dst) in enumerate(((tf_in, tf), (sp_in, sp), (sf_in, sf)))
    ]
    for copy in own:
        copy.start()
    loads = []
    for j in range(NZ):
        load = pltpu.make_async_copy(
            tp.at[pl.ds(pl.multiple_of((j * NY + y) * BLOCK, BLOCK), BLOCK), :], raw.at[pl.ds(j * BLOCK, BLOCK), :], raw_sem.at[j]
        )
        load.start()
        loads.append(load)

    def unit_into(src, dst, index):
        wide = src[...].astype(F32)
        dst[rows256(index), :] = (wide * inverse_length(wide)).astype(BF16)

    own[0].wait()
    unit_into(tf, tu, y)
    own[1].wait()
    unit_into(sp, st, z)
    pl.semaphore_wait(barrier, len(partners))

    def half_rows(index, part):
        return pl.ds(pl.multiple_of(index * BLOCK + part * (BLOCK // 2), BLOCK // 2), BLOCK // 2)

    t_copies = {}
    for d in (2, 1, 3):
        part = tu.at[half_rows(y, c), :]
        t_copies[d] = launch([remote(part, part, t_send.at[d], t_recv.at[d], at_y(d))])

    def ring(step):
        right, left = (z - step + 1 + NZ) % NZ, (z + step - 1) % NZ
        if step < 4:
            right_rows, left_rows = rows256(right), rows256(left)
        else:
            right_rows, left_rows = half_rows(right, 0), half_rows(left, 1)
        return launch([
            remote(st.at[right_rows, :], st.at[right_rows, :], ring_send.at[step, 0], ring_recv.at[step, 0], at_z(1)),
            remote(st.at[left_rows, :], st.at[left_rows, :], ring_send.at[step, 1], ring_recv.at[step, 1], at_z(NZ - 1)),
        ])

    ring_copies = ring(1)

    own[2].wait()
    unit_into(sf, su, y)

    for load in loads:
        load.wait()

    def table_step(i, _):
        rows = rows256(i)
        wide = raw[rows, :].astype(F32)
        tt[rows, :] = (wide * inverse_length(wide)).astype(BF16)
        return 0

    lax.fori_loop(0, NZ, table_step, 0, unroll=2)
    colacc[...] = jnp.zeros_like(colacc)

    def kernel_block(index):
        def step(j, _):
            cols = rows256(j)
            value = jnp.exp2(nt_dot(tu[rows256(index), :], tt[cols, :]) * TEACHER_EXP)
            kern[rows256(index), cols] = value
            colacc[:, cols] += fold8(value)
            return 0

        lax.fori_loop(0, NZ, step, 0, unroll=True)

    kernel_block(y)
    forwards = {}

    def forward(d):
        arrive(t_copies[d])
        part = tu.at[half_rows((y - d + NY) % NY, c), :]
        forwards[d] = launch([remote(part, part, f_send.at[d], f_recv.at[d], sibling)])

    forward(1)
    forward(3)
    arrive(forwards[1])
    kernel_block((y + NY - 1) % NY)
    forward(2)
    s_copies = launch([
        remote(su.at[rows256(y), :], su.at[rows256(y), :], s_send.at[d], s_recv.at[d], at_y(d)) for d in (2, 1, 3)
    ])
    arrive(forwards[3])
    kernel_block((y + NY - 3) % NY)
    arrive(ring_copies)
    ring_copies = ring(2)
    arrive(forwards[2])
    kernel_block((y + NY - 2) % NY)

    def student_block(offset):
        cols = rows256((z + offset + NZ) % NZ)

        def step(i, _):
            rows = rows256(i)
            value = nt_dot(su[rows, :], st[cols, :])
            score[rows, cols] = value
            power = jnp.exp2(value * STUDENT_EXP)
            expo[rows, cols] = power
            totacc[rows, :] += power[:, :LANES] + power[:, LANES:]
            return 0

        lax.fori_loop(0, NY, step, 0, unroll=True)

    def student_blocks(count, offset_of):
        def step(i, _):
            student_block(offset_of(i))
            return 0

        lax.fori_loop(0, count, step, 0)

    def student_crops():
        arrive(s_copies)
        totacc[...] = jnp.zeros_like(totacc)
        for i in range(NY):
            rows = pl.ds(i * BLOCK, BLOCK)
            sut[:, rows] = jnp.transpose(su[rows, :].astype(F32)).astype(BF16)

    def lane_sums(src, dst, base):
        for j in range(CROPS // LANES):
            block = jnp.transpose(src[pl.ds(j * LANES, LANES), :])
            dst[base + j : base + j + 1, :] = jnp.sum(block, axis=0, keepdims=True)

    def spread(values, dst):
        for j in range(CROPS // LANES):
            dst[pl.ds(j * LANES, LANES), :] = jnp.transpose(jnp.broadcast_to(values[j : j + 1, :], (LANES, LANES)))

    groups = PROTOS // LANES

    def column_pass():
        def step(i, acc):
            rows = pl.ds(pl.multiple_of(i * 32, 32), 32)
            scale = rcol[rows, :]
            return tuple(acc[g] + fold8(kern[rows, g * LANES : (g + 1) * LANES] * scale) for g in range(groups))

        acc = lax.fori_loop(0, CROPS // 32, step, tuple(jnp.zeros((8, LANES), F32) for _ in range(groups)), unroll=4)
        for g in range(groups):
            colacc[:, g * LANES : (g + 1) * LANES] = acc[g]

    def row_pass():
        def step(i, _):
            rows = pl.ds(pl.multiple_of(i * 64, 64), 64)
            acc = kern[rows, 0:LANES] * cvec[:, 0:LANES]
            for g in range(1, groups):
                acc += kern[rows, g * LANES : (g + 1) * LANES] * cvec[:, g * LANES : (g + 1) * LANES]
            rowacc[rows, :] = acc
            return 0

        lax.fori_loop(0, CROPS // 64, step, 0, unroll=4)

    def exchange(buf, me, send, recv, order, where):
        return launch([remote(buf.at[me], buf.at[me], send.at[d], recv.at[d], where(d)) for d in order])

    def total_of(buf, count):
        total = buf[0]
        for k in range(1, count):
            total += buf[k]
        return total

    for t in range(ROUNDS):
        if t:
            column_pass()
        sums = jnp.sum(colacc[...], axis=0, keepdims=True)
        for j in range(NZ):
            zbuf[t, z, j : j + 1, :] = sums[:, j * BLOCK : (j + 1) * BLOCK]
        copies = exchange(zbuf.at[t], z, z_send.at[t], z_recv.at[t], Z_ORDER, at_z)
        if t == 2:
            arrive(ring_copies)
            student_block(4)
        arrive(copies)
        scale = 1.0 / total_of(zbuf.at[t], NZ)
        for j in range(NZ):
            cvec[:, j * BLOCK : (j + 1) * BLOCK] = scale[j : j + 1, :]
        if t < 2:
            arrive(ring_copies)
            ring_copies = ring(3 + t)
        row_pass()
        last = t == ROUNDS - 1
        rb = rlast if last else rbuf.at[t]
        mine = y * NP + p
        lane_sums(rowacc, rb.at[mine], 0)
        if last:
            lane_sums(totacc, rb.at[mine], 8)
        copies = exchange(rb, mine, r_send.at[t], r_recv.at[t], XY_ORDER, at_xy)
        if t == 0:
            student_crops()
            student_blocks(3, lambda i: 7 + i)
        if t == 1:
            student_blocks(4, lambda i: 2 + i + i // 2)
        arrive(copies)
        sums = total_of(rb, NXY)
        if not last:
            spread(1.0 / sums, rcol)
        else:
            totals = sums[8:16, :]
            spread(GAIN / totals, acol)
            spread(GAIN / sums[0:8, :], bcol)

    def grad_rows(offset, first_row, count, cross):
        first = pl.multiple_of(((z + offset) % NZ) * BLOCK, BLOCK)

        def step(i, cross):
            rows = pl.ds(pl.multiple_of(first_row + i * 64, 64), 64)
            a, bb = acol[rows, :], bcol[rows, :]
            for h in range(BLOCK // LANES):
                cols = pl.ds(pl.multiple_of(first + h * LANES, LANES), LANES)
                target = kern[rows, cols] * cvec[:, cols] * bb
                grad[rows, cols] = (expo[rows, cols] * a - target).astype(BF16)
                cross += fold8(target * score[rows, cols])
            return cross

        return lax.fori_loop(0, count // 64, step, cross, unroll=4)

    def grad_blocks(count, offset_of, cross, first_row=0, rows=CROPS):
        return lax.fori_loop(0, count, lambda i, total: grad_rows(offset_of(i), first_row, rows, total), cross)

    def proto_blocks(count, offset_of):
        def step(i, _):
            proto_block(offset_of(i))
            return 0

        lax.fori_loop(0, count, step, 0)

    def proto_block(offset):
        cols = rows256((z + offset) % NZ)
        gp[offset] = jnp.dot(sut[...], grad[:, cols], preferred_element_type=F32)

    units = [
        (4, 0, 4, 1), (3, 1, 5, 0), (3, 0, 5, 1), (2, 1, 6, 0), (2, 0, 6, 1), (1, 1, 7, 0), (1, 0, 7, 1),
    ]
    right_way, left_way = at_z(1), at_z(NZ - 1)
    unit_copies = {}

    def piece(half, part):
        return pl.ds(half * HALF + part * PIECE, PIECE)

    def unit(k):
        ro, rh, lo, lh = units[k]
        for part in range(PARTS):
            at = pl.ds(part * PIECE, PIECE)
            mine_right, mine_left = gp.at[ro, piece(rh, part), :], gp.at[lo, piece(lh, part), :]
            if k < 2:
                own_right[k, at, :] = mine_right[...].astype(BF16)
                own_left[k, at, :] = mine_left[...].astype(BF16)
                pair = [(own_right.at[k, at, :], first_right.at[k, at, :]), (own_left.at[k, at, :], first_left.at[k, at, :])]
            else:
                arrive(unit_copies[k - 2, part])
                before_right, before_left = (first_right, first_left) if k < 4 else (rs_right, rs_left)
                mine_right[...] += before_right[k - 2, at, :].astype(F32)
                mine_left[...] += before_left[k - 2, at, :].astype(F32)
                pair = [(mine_right, rs_right.at[k, at, :]), (mine_left, rs_left.at[k, at, :])]
            unit_copies[k, part] = launch([
                remote(pair[0][0], pair[0][1], rs_send.at[k, part, 0], rs_recv.at[k, part, 0], right_way),
                remote(pair[1][0], pair[1][1], rs_send.at[k, part, 1], rs_recv.at[k, part, 1], left_way),
            ])

    cross = jnp.zeros((8, LANES), F32)
    cross = grad_rows(4, 0, CROPS, cross)
    proto_block(4)
    unit(0)
    cross = grad_blocks(2, lambda i: 3 + 2 * i, cross)
    proto_blocks(2, lambda i: 3 + 2 * i)
    unit(1)

    part_rows = BLOCK // NP
    sib, x_copies, y_copies, y_first = {}, {}, {}, {}

    def block_of(e):
        return (y + e) % NY

    def to_sibling(e):
        return remote(gu.at[block_of(e), 1 - c], gu_sib.at[e], sib_send.at[e], sib_recv.at[e], sibling)

    def crop_step(k, cross):
        e = (2 + 3 * k) % NY
        i = block_of(e)
        cross = grad_blocks(5, lambda n: (6 + n) % NZ, cross, pl.multiple_of(i * BLOCK, BLOCK), BLOCK)
        value = jnp.dot(grad[rows256(i), :], st[...], preferred_element_type=F32)
        gu[i] = value.reshape(NC, NX, part_rows, DIM)
        to_sibling(e).start()
        return cross

    cross = lax.fori_loop(0, 2, crop_step, cross)
    unit(2)
    cross = lax.fori_loop(2, NY, crop_step, cross)
    proto_blocks(2, lambda i: 2 + 4 * i)
    unit(3)
    for e in range(NY):
        sib[e] = [to_sibling(e)]
    flight.extend(copies[0] for copies in sib.values())

    upper, lower = pl.ds(0, part_rows // 2), pl.ds(part_rows // 2, part_rows // 2)

    def first_hop(e):
        i = block_of(e)
        arrive(sib[e])
        gu[i, c] += gu_sib[e]
        if e:
            y_first[e] = launch([
                remote(gu.at[i, c, :, lower, :], ybuf.at[e], yf_send.at[e], yf_recv.at[e], at_y(e))
            ])
        x_copies[e] = launch([
            remote(gu.at[i, c, (x + d) % NX, upper, :], xbuf.at[e, d], x_send.at[e, d], x_recv.at[e, d], at_x(d))
            for d in (2, 1, 3)
        ])

    def upper_over_y(e):
        i = block_of(e)
        arrive(x_copies[e])
        gu[i, c, x, upper, :] += xbuf[e, 1] + xbuf[e, 2] + xbuf[e, 3]
        if e:
            y_copies[e] = launch([
                remote(gu.at[i, c, x, upper, :], yred.at[e], yr_send.at[e], yr_recv.at[e], at_y(e))
            ])

    def lower_over_x():
        for e in (2, 1, 3):
            arrive(y_first[e])
        xall[x] = gu[y, c, :, lower, :] + ybuf[1] + ybuf[2] + ybuf[3]
        return exchange(xall, x, xr_send, xr_recv, (2, 1, 3), at_x)

    def finished(rows, grad_unit):
        wide = sf[rows, :].astype(F32)
        inverse = inverse_length(wide)
        direction = wide * inverse
        inner = jnp.sum(direction * grad_unit, axis=-1, keepdims=True)
        gs_out[rows, :] = (grad_unit - direction * inner) * inverse

    def half_part(k, half):
        size = part_rows // 2
        return pl.ds(pl.multiple_of(c * (BLOCK // 2) + k * part_rows + half * size, size), size)

    for e in (2, 1, 0, 3):
        first_hop(e)
    proto_blocks(3, lambda i: (7 + i) % NZ)
    lossp[mine] = jnp.log(totals) * (1.0 / NXY) - cross
    loss_copies = exchange(lossp, mine, lp_send, lp_recv, XY_ORDER, at_xy)
    unit(4)
    unit(5)
    x_last = lower_over_x()
    for e in (2, 1, 0, 3):
        upper_over_y(e)
    arrive(loss_copies)
    lossz[z] = total_of(lossp, NXY)
    loss_copies = exchange(lossz, z, lz_send, lz_recv, Z_ORDER, at_z)
    unit(6)
    for e in (2, 1, 3):
        arrive(y_copies[e])
    part = half_part(x, 0)
    finished(part, gu[y, c, x, upper, :] + yred[1] + yred[2] + yred[3])
    ag_copies = launch([
        remote(gs_out.at[part, :], gs_out.at[part, :], ag_send.at[d], ag_recv.at[d], at_p(d)) for d in P_ORDER
    ])
    arrive(x_last)
    low_copies = []
    for k in range(NX):
        rows = half_part(k, 1)
        finished(rows, xall[0, k] + xall[1, k] + xall[2, k] + xall[3, k])
        low_copies += launch([remote(gs_out.at[rows, :], gs_out.at[rows, :], low_send.at[k], low_recv.at[k], sibling)])
    for k in (5, 6):
        for part in range(PARTS):
            arrive(unit_copies[k, part])
            at = pl.ds(part * PIECE, PIECE)
            right_half, left_half = units[k][1], units[k][3]
            gp[0, piece(right_half, part), :] += rs_right[k, at, :]
            gp[0, piece(left_half, part), :] += rs_left[k, at, :]
    gp_out[...] = gp[0]
    arrive(loss_copies)
    loss_out[...] = total_of(lossz, NZ)
    arrive(low_copies)
    arrive(ag_copies)
    for copy in landed:
        copy.wait_send()


def finish(loss_parts, gs, gp, loss_out, gs_out, gp_out, loss_in, gs_in, gp_in, sem):
    copies = [
        pltpu.make_async_copy(gp, gp_in, sem.at[0]),
        pltpu.make_async_copy(gs, gs_in, sem.at[1]),
        pltpu.make_async_copy(loss_parts, loss_in, sem.at[2]),
    ]
    for copy in copies:
        copy.start()
    copies[0].wait()
    gp_out[...] = jnp.transpose(gp_in[...])
    copies[1].wait()
    gs_out[...] = gs_in[...]
    copies[2].wait()
    loss_out[...] = jnp.sum(loss_in[...], keepdims=True) * (1.0 / (NZ * NY * BLOCK))


def on_device(teacher_feat, student_feat, teacher_protos, student_protos):
    vmem, dma = pltpu.VMEM, pltpu.SemaphoreType.DMA
    part_rows = BLOCK // NP
    scratch = [
        *[vmem((BLOCK, DIM), BF16) for _ in range(3)],
        vmem((PROTOS, DIM), BF16), vmem((PROTOS, DIM), BF16), vmem((PROTOS, DIM), BF16),
        vmem((CROPS, DIM), BF16), vmem((CROPS, DIM), BF16), vmem((DIM, CROPS), BF16),
        vmem((CROPS, PROTOS), F32), vmem((CROPS, PROTOS), F32), vmem((CROPS, PROTOS), F32),
        vmem((CROPS, PROTOS), BF16), vmem((1, PROTOS), F32), vmem((8, PROTOS), F32),
        *[vmem((CROPS, LANES), F32) for _ in range(5)],
        vmem((ROUNDS, NZ, NZ, BLOCK), F32), vmem((ROUNDS - 1, NXY, 8, LANES), F32), vmem((NXY, 16, LANES), F32),
        vmem((NZ, DIM, BLOCK), F32), vmem((7, HALF, BLOCK), F32), vmem((7, HALF, BLOCK), F32),
        *[vmem((2, HALF, BLOCK), BF16) for _ in range(4)],
        vmem((NY, NC, NX, part_rows, DIM), F32), vmem((NY, NX, part_rows, DIM), F32),
        vmem((NY, NX, part_rows // 2, DIM), F32), vmem((NY, part_rows // 2, DIM), F32),
        vmem((NY, NX, part_rows // 2, DIM), F32), vmem((NX, NX, part_rows // 2, DIM), F32),
        vmem((NXY, 8, LANES), F32), vmem((NZ, 8, LANES), F32),
        dma((3,)), dma((NZ,)), dma((NY,)), dma((NY,)), dma((NY,)), dma((NY,)), dma((NY,)), dma((NY,)), dma((5, 2)), dma((5, 2)),
        dma((ROUNDS, NZ)), dma((ROUNDS, NZ)), dma((ROUNDS, NXY)), dma((ROUNDS, NXY)),
        dma((7, PARTS, 2)), dma((7, PARTS, 2)), dma((NY,)), dma((NY,)), dma((NY, NX)), dma((NY, NX)), *[dma((NY,)) for _ in range(4)], *[dma((NX,)) for _ in range(4)], dma((NP,)), dma((NP,)),
        dma((NXY,)), dma((NXY,)), dma((NZ,)), dma((NZ,)),
    ]
    whole, anywhere = pl.BlockSpec(memory_space=pltpu.VMEM), pl.BlockSpec(memory_space=pl.ANY)
    loss, grad_student, grad_protos = pl.pallas_call(
        body,
        out_shape=(
            jax.ShapeDtypeStruct((8, LANES), F32),
            jax.ShapeDtypeStruct((BLOCK, DIM), F32),
            jax.ShapeDtypeStruct((DIM, BLOCK), F32),
        ),
        in_specs=[anywhere] * 4,
        out_specs=(whole, whole, whole),
        scratch_shapes=scratch,
        compiler_params=pltpu.CompilerParams(
            collective_id=0, has_side_effects=True, vmem_limit_bytes=60 << 20
        ),
        name="sinkhorn_head",
    )(teacher_feat, student_feat, student_protos, teacher_protos)
    loss, grad_student, grad_protos = pl.pallas_call(
        finish,
        out_shape=(
            jax.ShapeDtypeStruct((1, 1), F32),
            jax.ShapeDtypeStruct((BLOCK, DIM), F32),
            jax.ShapeDtypeStruct((BLOCK, DIM), F32),
        ),
        in_specs=[anywhere, anywhere, anywhere],
        out_specs=(whole, whole, whole),
        scratch_shapes=[vmem((8, LANES), F32), vmem((BLOCK, DIM), F32), vmem((DIM, BLOCK), F32), dma((3,))],
        name="finish",
    )(loss, grad_student, grad_protos)
    return loss.reshape(()), grad_student, grad_protos


def solution(mesh):
    in_specs = (P("batch", None), P("batch", None), P("proto", None), P(("proto", "batch"), None))
    out_specs = (P(), P("batch", None), P(("proto", "batch"), None))
    return jax.shard_map(on_device, mesh=mesh, in_specs=in_specs, out_specs=out_specs, check_vma=False)
```

```python
import functools
import math

import jax
import jax.numpy as jnp
from jax import lax
from jax.experimental import pallas as pl
from jax.experimental.pallas import tpu as pltpu
from jax.sharding import PartitionSpec as P

MESH = pl.DeviceIdType.MESH
NZ, NY, NX, NC = 8, 4, 4, 2
NP = NX * NC
NXY = NY * NP
DIM = 384
BLOCK = 256
CROPS = NY * BLOCK
PROTOS = NZ * BLOCK
ROUNDS = 3
EPSILON = 1e-06
LOG2E = 1.4426950408889634
TEACHER_EXP = LOG2E / 0.07
STUDENT_EXP = LOG2E / 0.1
GAIN = 10.0
F32, BF16 = jnp.float32, jnp.bfloat16
LANES = 128
HALF = DIM // 2
PARTS = 1
PIECE = HALF // PARTS
Z_ORDER = (4, 3, 5, 2, 6, 1, 7)
P_ORDER = (4, 3, 5, 2, 6, 1, 7)
XY_ORDER = tuple(e * NP + d for e in (2, 1, 3, 0) for d in (4, 3, 5, 2, 6, 1, 7, 0) if e or d)


def nt_dot(left, right):
    return lax.dot_general(left, right, (((1,), (1,)), ((), ())), preferred_element_type=F32)


def inverse_length(wide):
    return 1.0 / jnp.sqrt(jnp.sum(wide * wide, axis=-1, keepdims=True) + EPSILON)


def fold8(value):
    rows, lanes = value.shape
    return jnp.sum(value.reshape(rows // 8, 8, lanes), axis=0)


def body(
    tf_in, sf_in, sp_in, tp,
    loss_out, gs_out, gp_out,
    tf, sf, sp, raw, tt, st, tu, su, sut, kern, expo, score, grad, cvec, colacc,
    rowacc, totacc, rcol, acol, bcol,
    zbuf, rbuf, rlast,
    gp, rs_right, rs_left, own_right, own_left, first_right, first_left, gu, gu_sib, xbuf, yred, ybuf, xall, lossp, lossz,
    in_sem, raw_sem, t_send, t_recv, f_send, f_recv, s_send, s_recv, ring_send, ring_recv,
    z_send, z_recv, r_send, r_recv,
    rs_send, rs_recv, sib_send, sib_recv, x_send, x_recv, yr_send, yr_recv, yf_send, yf_recv, xr_send, xr_recv, low_send, low_recv, ag_send, ag_recv,
    lp_send, lp_recv, lz_send, lz_recv,
):
    b, p = lax.axis_index("batch"), lax.axis_index("proto")
    z, y = b // NY, b % NY
    x, c = p // NC, p % NC

    def at_z(d):
        return (((z + d) % NZ) * NY + y, p)

    def at_y(d):
        return (z * NY + (y + d) % NY, p)

    def at_xy(d):
        return (z * NY + (y + d // NP) % NY, (p + d % NP) % NP)

    def at_x(d):
        return (b, ((x + d) % NX) * NC + c)

    def at_p(d):
        return (b, (p + d) % NP)

    sibling = (b, x * NC + 1 - c)

    def remote(src, dst, send, recv, where):
        return pltpu.make_async_remote_copy(
            src_ref=src, dst_ref=dst, send_sem=send, recv_sem=recv, device_id=where, device_id_type=MESH
        )

    def rows256(index):
        return pl.ds(pl.multiple_of(index * BLOCK, BLOCK), BLOCK)

    flight, landed = [], []

    def launch(copies):
        for copy in copies:
            copy.start()
        flight.extend(copies)
        return copies

    def arrive(copies):
        for copy in copies:
            copy.wait_recv()
            flight[:] = [other for other in flight if other is not copy]
        landed.extend(copies)

    barrier = pltpu.get_barrier_semaphore()
    partners = (
        [at_z(d) for d in range(1, NZ)] + [at_xy(d) for d in range(1, NXY)]
    )
    for where in partners:
        pl.semaphore_signal(barrier, inc=1, device_id=where, device_id_type=MESH)
    own = [
        pltpu.make_async_copy(src, dst, in_sem.at[k]) for k, (src, dst) in enumerate(((tf_in, tf), (sp_in, sp), (sf_in, sf)))
    ]
    for copy in own:
        copy.start()
    loads = []
    for j in range(NZ):
        load = pltpu.make_async_copy(
            tp.at[pl.ds(pl.multiple_of((j * NY + y) * BLOCK, BLOCK), BLOCK), :], raw.at[pl.ds(j * BLOCK, BLOCK), :], raw_sem.at[j]
        )
        load.start()
        loads.append(load)

    def unit_into(src, dst, index):
        wide = src[...].astype(F32)
        dst[rows256(index), :] = (wide * inverse_length(wide)).astype(BF16)

    own[0].wait()
    unit_into(tf, tu, y)
    pl.semaphore_wait(barrier, len(partners))

    def half_rows(index, part):
        return pl.ds(pl.multiple_of(index * BLOCK + part * (BLOCK // 2), BLOCK // 2), BLOCK // 2)

    t_copies = {}
    for d in (2, 1, 3):
        part = tu.at[half_rows(y, c), :]
        t_copies[d] = launch([remote(part, part, t_send.at[d], t_recv.at[d], at_y(d))])

    def ring(step):
        right, left = (z - step + 1 + NZ) % NZ, (z + step - 1) % NZ
        if step < 4:
            right_rows, left_rows = rows256(right), rows256(left)
        else:
            right_rows, left_rows = half_rows(right, 0), half_rows(left, 1)
        return launch([
            remote(st.at[right_rows, :], st.at[right_rows, :], ring_send.at[step, 0], ring_recv.at[step, 0], at_z(1)),
            remote(st.at[left_rows, :], st.at[left_rows, :], ring_send.at[step, 1], ring_recv.at[step, 1], at_z(NZ - 1)),
        ])

    own[1].wait()
    unit_into(sp, st, z)
    ring_copies = ring(1)

    own[2].wait()
    unit_into(sf, su, y)

    for load in loads:
        load.wait()

    def table_step(i, _):
        rows = rows256(i)
        wide = raw[rows, :].astype(F32)
        tt[rows, :] = (wide * inverse_length(wide)).astype(BF16)
        return 0

    lax.fori_loop(0, NZ, table_step, 0, unroll=2)
    colacc[...] = jnp.zeros_like(colacc)

    def kernel_block(index):
        def step(j, _):
            cols = rows256(j)
            value = jnp.exp2(nt_dot(tu[rows256(index), :], tt[cols, :]) * TEACHER_EXP)
            kern[rows256(index), cols] = value
            colacc[:, cols] += fold8(value)
            return 0

        lax.fori_loop(0, NZ, step, 0, unroll=True)

    kernel_block(y)
    forwards = {}

    def forward(d):
        arrive(t_copies[d])
        part = tu.at[half_rows((y - d + NY) % NY, c), :]
        forwards[d] = launch([remote(part, part, f_send.at[d], f_recv.at[d], sibling)])

    forward(1)
    forward(3)
    arrive(ring_copies)
    ring_copies = ring(2)
    arrive(forwards[1])
    kernel_block((y + NY - 1) % NY)
    forward(2)
    s_copies = launch([
        remote(su.at[rows256(y), :], su.at[rows256(y), :], s_send.at[d], s_recv.at[d], at_y(d)) for d in (2, 1, 3)
    ])
    arrive(forwards[3])
    kernel_block((y + NY - 3) % NY)
    arrive(forwards[2])
    kernel_block((y + NY - 2) % NY)

    def student_block(offset):
        cols = rows256((z + offset + NZ) % NZ)

        def step(i, _):
            rows = rows256(i)
            value = nt_dot(su[rows, :], st[cols, :])
            score[rows, cols] = value
            power = jnp.exp2(value * STUDENT_EXP)
            expo[rows, cols] = power
            totacc[rows, :] += power[:, :LANES] + power[:, LANES:]
            return 0

        lax.fori_loop(0, NY, step, 0, unroll=True)

    def student_blocks(count, offset_of):
        def step(i, _):
            student_block(offset_of(i))
            return 0

        lax.fori_loop(0, count, step, 0)

    def student_crops():
        arrive(s_copies)
        totacc[...] = jnp.zeros_like(totacc)
        for i in range(NY):
            rows = pl.ds(i * BLOCK, BLOCK)
            sut[:, rows] = jnp.transpose(su[rows, :].astype(F32)).astype(BF16)

    def lane_sums(src, dst, base):
        for j in range(CROPS // LANES):
            block = jnp.transpose(src[pl.ds(j * LANES, LANES), :])
            dst[base + j : base + j + 1, :] = jnp.sum(block, axis=0, keepdims=True)

    def spread(values, dst):
        for j in range(CROPS // LANES):
            dst[pl.ds(j * LANES, LANES), :] = jnp.transpose(jnp.broadcast_to(values[j : j + 1, :], (LANES, LANES)))

    groups = PROTOS // LANES

    def column_pass():
        def step(i, acc):
            rows = pl.ds(pl.multiple_of(i * 32, 32), 32)
            scale = rcol[rows, :]
            return tuple(acc[g] + fold8(kern[rows, g * LANES : (g + 1) * LANES] * scale) for g in range(groups))

        acc = lax.fori_loop(0, CROPS // 32, step, tuple(jnp.zeros((8, LANES), F32) for _ in range(groups)), unroll=4)
        for g in range(groups):
            colacc[:, g * LANES : (g + 1) * LANES] = acc[g]

    def row_pass():
        def step(i, _):
            rows = pl.ds(pl.multiple_of(i * 64, 64), 64)
            acc = kern[rows, 0:LANES] * cvec[:, 0:LANES]
            for g in range(1, groups):
                acc += kern[rows, g * LANES : (g + 1) * LANES] * cvec[:, g * LANES : (g + 1) * LANES]
            rowacc[rows, :] = acc
            return 0

        lax.fori_loop(0, CROPS // 64, step, 0, unroll=4)

    def exchange(buf, me, send, recv, order, where):
        return launch([remote(buf.at[me], buf.at[me], send.at[d], recv.at[d], where(d)) for d in order])

    def total_of(buf, count):
        total = buf[0]
        for k in range(1, count):
            total += buf[k]
        return total

    for t in range(ROUNDS):
        if t:
            column_pass()
        sums = jnp.sum(colacc[...], axis=0, keepdims=True)
        for j in range(NZ):
            zbuf[t, z, j : j + 1, :] = sums[:, j * BLOCK : (j + 1) * BLOCK]
        copies = exchange(zbuf.at[t], z, z_send.at[t], z_recv.at[t], Z_ORDER, at_z)
        if t == 2:
            arrive(ring_copies)
            student_block(4)
        arrive(copies)
        scale = 1.0 / total_of(zbuf.at[t], NZ)
        for j in range(NZ):
            cvec[:, j * BLOCK : (j + 1) * BLOCK] = scale[j : j + 1, :]
        if t < 2:
            arrive(ring_copies)
            ring_copies = ring(3 + t)
        row_pass()
        last = t == ROUNDS - 1
        rb = rlast if last else rbuf.at[t]
        mine = y * NP + p
        lane_sums(rowacc, rb.at[mine], 0)
        if last:
            lane_sums(totacc, rb.at[mine], 8)
        copies = exchange(rb, mine, r_send.at[t], r_recv.at[t], XY_ORDER, at_xy)
        if t == 0:
            student_crops()
            student_blocks(3, lambda i: 7 + i)
        if t == 1:
            student_blocks(4, lambda i: 2 + i + i // 2)
        arrive(copies)
        sums = total_of(rb, NXY)
        if not last:
            spread(1.0 / sums, rcol)
        else:
            totals = sums[8:16, :]
            spread(GAIN / totals, acol)
            spread(GAIN / sums[0:8, :], bcol)

    def grad_rows(offset, first_row, count, cross):
        first = pl.multiple_of(((z + offset) % NZ) * BLOCK, BLOCK)

        def step(i, cross):
            rows = pl.ds(pl.multiple_of(first_row + i * 64, 64), 64)
            a, bb = acol[rows, :], bcol[rows, :]
            for h in range(BLOCK // LANES):
                cols = pl.ds(pl.multiple_of(first + h * LANES, LANES), LANES)
                target = kern[rows, cols] * cvec[:, cols] * bb
                grad[rows, cols] = (expo[rows, cols] * a - target).astype(BF16)
                cross += fold8(target * score[rows, cols])
            return cross

        return lax.fori_loop(0, count // 64, step, cross, unroll=4)

    def grad_blocks(count, offset_of, cross, first_row=0, rows=CROPS):
        return lax.fori_loop(0, count, lambda i, total: grad_rows(offset_of(i), first_row, rows, total), cross)

    def proto_blocks(count, offset_of):
        def step(i, _):
            proto_block(offset_of(i))
            return 0

        lax.fori_loop(0, count, step, 0)

    def proto_block(offset):
        cols = rows256((z + offset) % NZ)
        gp[offset] = jnp.dot(sut[...], grad[:, cols], preferred_element_type=F32)

    units = [
        (4, 0, 4, 1), (3, 1, 5, 0), (3, 0, 5, 1), (2, 1, 6, 0), (2, 0, 6, 1), (1, 1, 7, 0), (1, 0, 7, 1),
    ]
    right_way, left_way = at_z(1), at_z(NZ - 1)
    unit_copies = {}

    def piece(half, part):
        return pl.ds(half * HALF + part * PIECE, PIECE)

    def unit(k):
        ro, rh, lo, lh = units[k]
        for part in range(PARTS):
            at = pl.ds(part * PIECE, PIECE)
            mine_right, mine_left = gp.at[ro, piece(rh, part), :], gp.at[lo, piece(lh, part), :]
            if k < 2:
                own_right[k, at, :] = mine_right[...].astype(BF16)
                own_left[k, at, :] = mine_left[...].astype(BF16)
                pair = [(own_right.at[k, at, :], first_right.at[k, at, :]), (own_left.at[k, at, :], first_left.at[k, at, :])]
            else:
                arrive(unit_copies[k - 2, part])
                before_right, before_left = (first_right, first_left) if k < 4 else (rs_right, rs_left)
                mine_right[...] += before_right[k - 2, at, :].astype(F32)
                mine_left[...] += before_left[k - 2, at, :].astype(F32)
                pair = [(mine_right, rs_right.at[k, at, :]), (mine_left, rs_left.at[k, at, :])]
            unit_copies[k, part] = launch([
                remote(pair[0][0], pair[0][1], rs_send.at[k, part, 0], rs_recv.at[k, part, 0], right_way),
                remote(pair[1][0], pair[1][1], rs_send.at[k, part, 1], rs_recv.at[k, part, 1], left_way),
            ])

    cross = jnp.zeros((8, LANES), F32)
    cross = grad_rows(4, 0, CROPS, cross)
    proto_block(4)
    unit(0)
    cross = grad_blocks(2, lambda i: 3 + 2 * i, cross)
    proto_blocks(2, lambda i: 3 + 2 * i)
    unit(1)

    part_rows = BLOCK // NP
    sib, x_copies, y_copies, y_first = {}, {}, {}, {}

    def block_of(e):
        return (y + e) % NY

    def to_sibling(e):
        return remote(gu.at[block_of(e), 1 - c], gu_sib.at[e], sib_send.at[e], sib_recv.at[e], sibling)

    def crop_step(k, cross):
        e = (2 + 3 * k) % NY
        i = block_of(e)
        cross = grad_blocks(5, lambda n: (6 + n) % NZ, cross, pl.multiple_of(i * BLOCK, BLOCK), BLOCK)
        value = jnp.dot(grad[rows256(i), :], st[...], preferred_element_type=F32)
        gu[i] = value.reshape(NC, NX, part_rows, DIM)
        to_sibling(e).start()
        return cross

    cross = lax.fori_loop(0, 2, crop_step, cross)
    unit(2)
    cross = lax.fori_loop(2, NY, crop_step, cross)
    proto_blocks(2, lambda i: 2 + 4 * i)
    unit(3)
    for e in range(NY):
        sib[e] = [to_sibling(e)]
    flight.extend(copies[0] for copies in sib.values())

    upper, lower = pl.ds(0, part_rows // 2), pl.ds(part_rows // 2, part_rows // 2)

    def first_hop(e):
        i = block_of(e)
        arrive(sib[e])
        gu[i, c] += gu_sib[e]
        if e:
            y_first[e] = launch([
                remote(gu.at[i, c, :, lower, :], ybuf.at[e], yf_send.at[e], yf_recv.at[e], at_y(e))
            ])
        x_copies[e] = launch([
            remote(gu.at[i, c, (x + d) % NX, upper, :], xbuf.at[e, d], x_send.at[e, d], x_recv.at[e, d], at_x(d))
            for d in (2, 1, 3)
        ])

    def upper_over_y(e):
        i = block_of(e)
        arrive(x_copies[e])
        gu[i, c, x, upper, :] += xbuf[e, 1] + xbuf[e, 2] + xbuf[e, 3]
        if e:
            y_copies[e] = launch([
                remote(gu.at[i, c, x, upper, :], yred.at[e], yr_send.at[e], yr_recv.at[e], at_y(e))
            ])

    def lower_over_x():
        for e in (2, 1, 3):
            arrive(y_first[e])
        xall[x] = gu[y, c, :, lower, :] + ybuf[1] + ybuf[2] + ybuf[3]
        return exchange(xall, x, xr_send, xr_recv, (2, 1, 3), at_x)

    def finished(rows, grad_unit):
        wide = sf[rows, :].astype(F32)
        inverse = inverse_length(wide)
        direction = wide * inverse
        inner = jnp.sum(direction * grad_unit, axis=-1, keepdims=True)
        gs_out[rows, :] = (grad_unit - direction * inner) * inverse

    def half_part(k, half):
        size = part_rows // 2
        return pl.ds(pl.multiple_of(c * (BLOCK // 2) + k * part_rows + half * size, size), size)

    for e in (2, 1, 3, 0):
        first_hop(e)
    proto_blocks(3, lambda i: (7 + i) % NZ)
    lossp[mine] = jnp.log(totals) * (1.0 / NXY) - cross
    loss_copies = exchange(lossp, mine, lp_send, lp_recv, XY_ORDER, at_xy)
    unit(4)
    unit(5)
    for e in (2, 1, 3):
        upper_over_y(e)
    x_last = lower_over_x()
    upper_over_y(0)
    arrive(loss_copies)
    lossz[z] = total_of(lossp, NXY)
    loss_copies = exchange(lossz, z, lz_send, lz_recv, Z_ORDER, at_z)
    unit(6)
    for e in (2, 1, 3):
        arrive(y_copies[e])
    part = half_part(x, 0)
    finished(part, gu[y, c, x, upper, :] + yred[1] + yred[2] + yred[3])
    ag_copies = launch([
        remote(gs_out.at[part, :], gs_out.at[part, :], ag_send.at[d], ag_recv.at[d], at_p(d)) for d in P_ORDER
    ])
    arrive(x_last)
    low_copies = []
    for k in range(NX):
        rows = half_part(k, 1)
        finished(rows, xall[0, k] + xall[1, k] + xall[2, k] + xall[3, k])
        low_copies += launch([remote(gs_out.at[rows, :], gs_out.at[rows, :], low_send.at[k], low_recv.at[k], sibling)])
    for k in (5, 6):
        for part in range(PARTS):
            arrive(unit_copies[k, part])
            at = pl.ds(part * PIECE, PIECE)
            right_half, left_half = units[k][1], units[k][3]
            gp[0, piece(right_half, part), :] += rs_right[k, at, :]
            gp[0, piece(left_half, part), :] += rs_left[k, at, :]
    gp_out[...] = gp[0]
    arrive(loss_copies)
    loss_out[...] = total_of(lossz, NZ)
    arrive(low_copies)
    arrive(ag_copies)
    for copy in landed:
        copy.wait_send()


def finish(loss_parts, gs, gp, loss_out, gs_out, gp_out, loss_in, gs_in, gp_in, sem):
    copies = [
        pltpu.make_async_copy(gp, gp_in, sem.at[0]),
        pltpu.make_async_copy(gs, gs_in, sem.at[1]),
        pltpu.make_async_copy(loss_parts, loss_in, sem.at[2]),
    ]
    for copy in copies:
        copy.start()
    copies[0].wait()
    gp_out[...] = jnp.transpose(gp_in[...])
    copies[1].wait()
    gs_out[...] = gs_in[...]
    copies[2].wait()
    loss_out[...] = jnp.sum(loss_in[...], keepdims=True) * (1.0 / (NZ * NY * BLOCK))


def on_device(teacher_feat, student_feat, teacher_protos, student_protos):
    vmem, dma = pltpu.VMEM, pltpu.SemaphoreType.DMA
    part_rows = BLOCK // NP
    scratch = [
        *[vmem((BLOCK, DIM), BF16) for _ in range(3)],
        vmem((PROTOS, DIM), BF16), vmem((PROTOS, DIM), BF16), vmem((PROTOS, DIM), BF16),
        vmem((CROPS, DIM), BF16), vmem((CROPS, DIM), BF16), vmem((DIM, CROPS), BF16),
        vmem((CROPS, PROTOS), F32), vmem((CROPS, PROTOS), F32), vmem((CROPS, PROTOS), F32),
        vmem((CROPS, PROTOS), BF16), vmem((1, PROTOS), F32), vmem((8, PROTOS), F32),
        *[vmem((CROPS, LANES), F32) for _ in range(5)],
        vmem((ROUNDS, NZ, NZ, BLOCK), F32), vmem((ROUNDS - 1, NXY, 8, LANES), F32), vmem((NXY, 16, LANES), F32),
        vmem((NZ, DIM, BLOCK), F32), vmem((7, HALF, BLOCK), F32), vmem((7, HALF, BLOCK), F32),
        *[vmem((2, HALF, BLOCK), BF16) for _ in range(4)],
        vmem((NY, NC, NX, part_rows, DIM), F32), vmem((NY, NX, part_rows, DIM), F32),
        vmem((NY, NX, part_rows // 2, DIM), F32), vmem((NY, part_rows // 2, DIM), F32),
        vmem((NY, NX, part_rows // 2, DIM), F32), vmem((NX, NX, part_rows // 2, DIM), F32),
        vmem((NXY, 8, LANES), F32), vmem((NZ, 8, LANES), F32),
        dma((3,)), dma((NZ,)), dma((NY,)), dma((NY,)), dma((NY,)), dma((NY,)), dma((NY,)), dma((NY,)), dma((5, 2)), dma((5, 2)),
        dma((ROUNDS, NZ)), dma((ROUNDS, NZ)), dma((ROUNDS, NXY)), dma((ROUNDS, NXY)),
        dma((7, PARTS, 2)), dma((7, PARTS, 2)), dma((NY,)), dma((NY,)), dma((NY, NX)), dma((NY, NX)), *[dma((NY,)) for _ in range(4)], *[dma((NX,)) for _ in range(4)], dma((NP,)), dma((NP,)),
        dma((NXY,)), dma((NXY,)), dma((NZ,)), dma((NZ,)),
    ]
    whole, anywhere = pl.BlockSpec(memory_space=pltpu.VMEM), pl.BlockSpec(memory_space=pl.ANY)
    loss, grad_student, grad_protos = pl.pallas_call(
        body,
        out_shape=(
            jax.ShapeDtypeStruct((8, LANES), F32),
            jax.ShapeDtypeStruct((BLOCK, DIM), F32),
            jax.ShapeDtypeStruct((DIM, BLOCK), F32),
        ),
        in_specs=[anywhere] * 4,
        out_specs=(whole, whole, whole),
        scratch_shapes=scratch,
        compiler_params=pltpu.CompilerParams(
            collective_id=0, has_side_effects=True, vmem_limit_bytes=60 << 20
        ),
        name="sinkhorn_head",
    )(teacher_feat, student_feat, student_protos, teacher_protos)
    loss, grad_student, grad_protos = pl.pallas_call(
        finish,
        out_shape=(
            jax.ShapeDtypeStruct((1, 1), F32),
            jax.ShapeDtypeStruct((BLOCK, DIM), F32),
            jax.ShapeDtypeStruct((BLOCK, DIM), F32),
        ),
        in_specs=[anywhere, anywhere, anywhere],
        out_specs=(whole, whole, whole),
        scratch_shapes=[vmem((8, LANES), F32), vmem((BLOCK, DIM), F32), vmem((DIM, BLOCK), F32), dma((3,))],
        name="finish",
    )(loss, grad_student, grad_protos)
    return loss.reshape(()), grad_student, grad_protos


def solution(mesh):
    in_specs = (P("batch", None), P("batch", None), P("proto", None), P(("proto", "batch"), None))
    out_specs = (P(), P("batch", None), P(("proto", "batch"), None))
    return jax.shard_map(on_device, mesh=mesh, in_specs=in_specs, out_specs=out_specs, check_vma=False)
```
